1024 devices in a mesh: fsdp: 32 (over z_lo, x, core), rep: 32 (over y, z_hi).
Axes of the slice: x: 4, y: 8, z: 16 (z_hi: 4, z_lo: 4; z = z_hi * 4 + z_lo), core: 2. Of those that a mesh axis runs over, the one named last changes fastest.
Arguments:
- gradients: bfloat16 [32, 32, 32, 16, 2048], P('rep', 'fsdp'), may hold values from -1.1953125 to 1.1953125
- second_moment: float32 [32, 32, 16, 2048], P('fsdp', 'rep'), may hold values from 0.02 to 5
- left_rows: bfloat16 [32, 32, 64, 512], P('rep', 'fsdp'), may hold values from -1 to 2
- right_root: bfloat16 [32, 4, 512, 512], P('rep'), may hold values from -1 to 2
- owner_table: int32 [32, 32], replicated, may hold values from 0 to 31, as said below
- step_count: int32 [1], replicated, may hold values from 1 to 40
Outputs:
- update: bfloat16 [32, 32, 16, 2048], P('fsdp', 'rep')
- new_moment: float32 [32, 32, 16, 2048], P('fsdp', 'rep')
The draws below stay inside these ranges and needn't reach their ends.
Inputs may be any that keep to these rules, and one draw needn't show every extreme that they name: `owner_table`: each row is a permutation of the work items' workers.
All inputs are finite; a program needn't handle non-finite values.
Results may differ from the reference program's by a relative error of at most 0.024.
Values may be sent and summed in bfloat16 or wider, within the bound.
No kernel may reach another device: no remote copies, remote signals or barrier semaphores. Data moves between devices by JAX's collectives and lax.ppermute only.
A program may use at most 32 MiB of HBM per device.

```python
import math
import jax
import jax.numpy as jnp
from jax import lax

BLOCK = 512
GB = 4
SUB = 16
TEAM = 8
SHARE = 2
N_FSDP = 32
N_REP = 32


def shared_owners(key):
    group_keys = jax.random.split(key, N_REP)
    return jax.vmap(lambda subkey: jax.random.permutation(subkey, N_FSDP))(group_keys).astype(jnp.int32)


def symmetric_root(noise_vals, diag_key):
    diag_vals = jax.random.uniform(diag_key, (N_REP, GB, BLOCK), jnp.float32, 0.7, 1.5)
    row_ids = lax.broadcasted_iota(jnp.int32, (BLOCK, BLOCK), 0)
    col_ids = lax.broadcasted_iota(jnp.int32, (BLOCK, BLOCK), 1)
    identity = (row_ids == col_ids).astype(jnp.float32)
    coef = 0.3 * (0.5 / BLOCK) ** 0.5
    return coef * (noise_vals + jnp.swapaxes(noise_vals, -1, -2)) + diag_vals[..., None] * identity


def draw_owner_table(key, part):
    owner_rows = shared_owners(key)
    return owner_rows


def draw_left_rows(key, part):
    owner_rows = shared_owners(key)
    key = jax.random.fold_in(key, 5)
    noise_key, diag_key = jax.random.split(key)
    full_shape = (N_REP, GB, BLOCK, BLOCK)
    noise_vals = jnp.clip(jax.random.normal(noise_key, full_shape, jnp.float32), -6.0, 6.0)
    full_matrix = symmetric_root(noise_vals, diag_key)
    item_rows = full_matrix.reshape(N_REP, GB, N_FSDP, TEAM, SHARE, BLOCK).transpose(0, 1, 3, 2, 4, 5).reshape(N_REP, N_FSDP, N_FSDP * SHARE, BLOCK)
    inverse = jnp.argsort(owner_rows, axis=1, stable=True)
    return jnp.take_along_axis(item_rows, inverse[:, :, None, None], axis=1).astype(jnp.bfloat16)


def draw_right_root(key, part):
    key = jax.random.fold_in(key, 7)
    noise_key, diag_key = jax.random.split(key)
    full_shape = (N_REP, GB, BLOCK, BLOCK)
    noise_vals = jnp.clip(jax.random.normal(noise_key, full_shape, jnp.float32), -6.0, 6.0)
    return symmetric_root(noise_vals, diag_key).astype(jnp.bfloat16)


def draw_second_moment(key, part):
    key = jax.random.fold_in(key, 9)
    full_shape = (N_FSDP, N_REP, SUB, GB * BLOCK)
    position = lax.broadcasted_iota(jnp.float32, full_shape, 0) / max(N_FSDP - 1, 1)
    base_vals = jnp.exp(jax.random.uniform(key, full_shape, jnp.float32, math.log(0.2), math.log(5.0)))
    ramp_vals = jnp.exp(-math.log(3.0) * position)
    return base_vals * ramp_vals


def with_spikes(values, own_key, source, target, blocks, factor):
    def block_of(dim):
        return (jnp.arange(values.shape[dim]) // (values.shape[dim] // blocks)).reshape((-1,) + (1,) * (values.ndim - 1 - dim))

    near = jax.random.permutation(own_key, blocks)[block_of(target)]
    other_side = (block_of(target) + blocks // 2) % blocks
    return jnp.where((block_of(source) == near) | (block_of(source) == other_side), factor * values, values)


def levels(rng, extent, shards, smallest, largest):
    level = 1.0
    for dim, shards_of in shards:
        draws = jax.random.uniform(jax.random.fold_in(jax.random.fold_in(rng, 6), dim), (shards_of,), jnp.float32, smallest / len(shards), largest / len(shards))
        level = level * jnp.repeat(jnp.exp(draws), extent[dim] // shards_of).reshape((-1,) + (1,) * (len(extent) - 1 - dim))
    return level


def heavy_noise(own_key, dims, width, limit, pieces, heavy, kind=jnp.bfloat16):
    result = width * jax.random.normal(own_key, dims, jnp.float32)
    if pieces:
        result = result * levels(own_key, dims, pieces, -0.22, 0.18)
    return jnp.clip(with_spikes(result, jax.random.fold_in(own_key, 3), *heavy), -limit, limit).astype(kind)


def setup_inputs(seed: int = 0) -> dict:
    key_list = jax.random.split(jax.random.key(seed), 7)
    gradients = heavy_noise(key_list[0], (N_REP, N_FSDP, N_REP, SUB, GB * BLOCK), 0.2, 1.1953125, ((0, 32), (1, 32)), (0, 2, 32, 2.75))
    second_moment = draw_second_moment(jax.random.fold_in(key_list[6], 71), 0)
    left_rows = draw_left_rows(jax.random.fold_in(key_list[6], 71), 0)
    right_root = draw_right_root(jax.random.fold_in(key_list[6], 71), 0)
    owner_table = draw_owner_table(jax.random.fold_in(key_list[6], 71), 0)
    step_count = jax.random.randint(key_list[5], (1,), 1, 41).astype(jnp.int32)
    return {"gradients": gradients, "second_moment": second_moment, "left_rows": left_rows, "right_root": right_root, "owner_table": owner_table, "step_count": step_count}


beta_two = 0.95
adam_eps = 1e-08

def reference(gradients, second_moment, left_rows, right_root, owner_table, step_count):

    def add_replica(replica, running):
        return running + lax.dynamic_index_in_dim(gradients, replica, 0, keepdims=False).astype(jnp.float32)
    summed = lax.fori_loop(0, N_REP, add_replica, jnp.zeros(gradients.shape[1:], jnp.float32))
    step_value = step_count[0].astype(jnp.float32)
    correction = 1.0 - jnp.power(jnp.float32(beta_two), step_value)
    new_moment = beta_two * second_moment + (1.0 - beta_two) * summed * summed
    adam_dir = summed / (jnp.sqrt(new_moment / correction) + adam_eps)
    adam_sq = lax.optimization_barrier(jnp.sum((adam_dir * adam_dir).reshape(N_FSDP, N_REP, SUB, GB, BLOCK), axis=(0, 2, 4)))
    grad_bf = summed.astype(jnp.bfloat16)
    blocks_all = grad_bf.reshape(N_FSDP, N_REP, SUB, GB, BLOCK).transpose(1, 3, 0, 2, 4).reshape(N_REP, GB, BLOCK, BLOCK)

    def per_group(inputs):
        grad_group, left_group, right_group, owner_row, adam_group = inputs
        item_rows = jnp.take(left_group, owner_row, axis=0)
        left_mat = item_rows.reshape(GB, TEAM, N_FSDP, SHARE, BLOCK).transpose(0, 2, 1, 3, 4).reshape(GB, BLOCK, BLOCK)
        first_product = jnp.einsum('kab,kbc->kac', left_mat.astype(jnp.float32), grad_group.astype(jnp.float32)).astype(jnp.bfloat16)
        precond = jnp.einsum('kab,kbc->kac', first_product.astype(jnp.float32), right_group.astype(jnp.float32))
        precond_sq = lax.optimization_barrier(jnp.sum(precond * precond, axis=(1, 2)))
        graft_ratio = jnp.sqrt(adam_group / (precond_sq + 1e-06))
        return (precond * graft_ratio[:, None, None]).astype(jnp.bfloat16)
    updates = lax.map(per_group, (blocks_all, left_rows, right_root, owner_table, adam_sq))
    update = updates.reshape(N_REP, GB, N_FSDP, SUB, BLOCK).transpose(2, 0, 3, 1, 4).reshape(N_FSDP, N_REP, SUB, GB * BLOCK)
    return (update, new_moment)
```

```python
import jax
import jax.numpy as jnp
from jax import lax
from jax.experimental import pallas as pl
from jax.experimental.pallas import tpu as pltpu
from jax.sharding import Mesh, PartitionSpec as P

beta_two = 0.95
adam_eps = 1e-08
FS = ("z_lo", "x", "core")
REP = ("y", "z_hi")
f32 = jnp.float32
bf16 = jnp.bfloat16
VMEM_LIMIT = 32 * 1024 * 1024


def params():
    return pltpu.CompilerParams(vmem_limit_bytes=VMEM_LIMIT)


def ring_first(chunks, index, received, keep_low):
    _, parts, rows, width = chunks.shape
    half = parts // 2

    def body(idx, own, got, out):
        if keep_low:
            out[:half] = (own[0, :half].astype(f32) + got[...].astype(f32)).astype(bf16)
            out[half:] = own[0, half:]
        else:
            out[half:] = (own[0, half:].astype(f32) + got[...].astype(f32)).astype(bf16)
            out[:half] = own[0, :half]

    return pl.pallas_call(
        body,
        grid_spec=pltpu.PrefetchScalarGridSpec(
            num_scalar_prefetch=1,
            grid=(1,),
            in_specs=[
                pl.BlockSpec((1, parts, rows, width), lambda i, idx: (idx[0], 0, 0, 0)),
                pl.BlockSpec((half, rows, width), lambda i, idx: (0, 0, 0)),
            ],
            out_specs=pl.BlockSpec((parts, rows, width), lambda i, idx: (0, 0, 0)),
        ),
        out_shape=jax.ShapeDtypeStruct((parts, rows, width), bf16),
        compiler_params=params(),
        name="ring_first",
    )(index, chunks, received)


def ring_add(chunks, index, *received):
    _, parts, rows, width = chunks.shape
    piece = parts // 2

    def body(idx, own, *refs):
        total = own[0].astype(f32)
        for got in refs[:-1]:
            total = total + got[...].astype(f32)
        refs[-1][...] = total.astype(bf16)

    block = pl.BlockSpec((piece, rows, width), lambda i, idx: (i, 0, 0))
    return pl.pallas_call(
        body,
        grid_spec=pltpu.PrefetchScalarGridSpec(
            num_scalar_prefetch=1,
            grid=(parts // piece,),
            in_specs=[pl.BlockSpec((1, piece, rows, width), lambda i, idx: (idx[0], i, 0, 0))]
            + [block] * len(received),
            out_specs=block,
        ),
        out_shape=jax.ShapeDtypeStruct((parts, rows, width), bf16),
        compiler_params=params(),
        name="ring_add",
    )(index, chunks, *received)


def right_product(parts, right):
    count, rows, width = parts.shape
    blocks, size, _ = right.shape
    tiles = size // 128

    def body(got, root, summed, pieces):
        total = got[0].astype(f32)
        for i in range(1, count):
            total = total + got[i].astype(f32)
        summed[...] = total
        grad = total.astype(bf16)
        for k in range(blocks):
            prod = jnp.dot(
                grad[:, k * size : (k + 1) * size], root[k], preferred_element_type=f32
            ).astype(bf16)
            for x in range(tiles):
                tile = prod[:, x * 128 : (x + 1) * 128]
                for c in range(2):
                    pieces[(k * tiles + x) * 2 + c] = tile

    return pl.pallas_call(
        body,
        out_shape=(
            jax.ShapeDtypeStruct((rows, width), f32),
            jax.ShapeDtypeStruct((blocks * tiles * 2, rows, 128), bf16),
        ),
        compiler_params=params(),
        name="right_product",
    )(parts, right)


def adam_part(summed, moment, correction, blocks):
    rows, width = summed.shape
    size = width // blocks

    def body(corr, grad, old, new, squares):
        g = grad[...]
        m = beta_two * old[...] + (1.0 - beta_two) * g * g
        new[...] = m
        d = g / (jnp.sqrt(m / corr[0]) + adam_eps)
        d = d * d
        lane = lax.broadcasted_iota(jnp.int32, (8, 128), 1)
        acc = jnp.zeros((8, 128), f32)
        for k in range(blocks):
            acc = jnp.where(lane == k, jnp.sum(d[:, k * size : (k + 1) * size]), acc)
        squares[...] = acc

    return pl.pallas_call(
        body,
        in_specs=[
            pl.BlockSpec(memory_space=pltpu.SMEM),
            pl.BlockSpec(memory_space=pltpu.VMEM),
            pl.BlockSpec(memory_space=pltpu.VMEM),
        ],
        out_shape=(
            jax.ShapeDtypeStruct((rows, width), f32),
            jax.ShapeDtypeStruct((8, 128), f32),
        ),
        compiler_params=params(),
        name="adam_part",
    )(correction, summed, moment)


def left_product(left, columns, squares, my_block, members, blocks):
    out_rows, size = left.shape

    def body(block, lref, cref, sref, out):
        prod = jnp.dot(lref[...], cref[...], preferred_element_type=f32)
        lane = lax.broadcasted_iota(jnp.int32, (8, 128), 1)
        row = lax.broadcasted_iota(jnp.int32, (8, 128), 0)
        norms = jnp.where(lane == blocks + block[0], jnp.sum(prod * prod), sref[...])
        high = norms.astype(bf16).astype(f32)
        rest = norms - high
        mid = rest.astype(bf16).astype(f32)
        low = rest - mid
        tail = jnp.where(row == 0, high, jnp.where(row == 1, mid, jnp.where(row == 2, low, 0.0)))
        out[:, :8, :] = prod.reshape(members, 8, 128).astype(bf16)
        out[:, 8:, :] = jnp.broadcast_to(tail[None], (members, 8, 128)).astype(bf16)

    return pl.pallas_call(
        body,
        in_specs=[pl.BlockSpec(memory_space=pltpu.SMEM)]
        + [pl.BlockSpec(memory_space=pltpu.VMEM)] * 3,
        out_shape=jax.ShapeDtypeStruct((members, 16, 128), bf16),
        compiler_params=params(),
        name="left_product",
    )(my_block, left, columns, squares)


def finish(returned, rows, width, blocks):
    members = returned.shape[0]
    tiles = members // blocks // 2

    def body(got, out):
        sums = jnp.sum(got[:, 8:, :].astype(f32), axis=0)
        sums = jnp.sum(sums, axis=0, keepdims=True)
        lane = lax.broadcasted_iota(jnp.int32, (1, 128), 1)
        for k in range(blocks):
            adam = jnp.sum(jnp.where(lane == k, sums, 0.0), axis=1, keepdims=True)
            shampoo = jnp.sum(jnp.where(lane == blocks + k, sums, 0.0), axis=1, keepdims=True)
            ratio = jnp.sqrt(adam / (shampoo + 1e-06))
            for x in range(tiles):
                d = (k * tiles + x) * 2
                both = jnp.concatenate([got[d, :8, :].astype(f32), got[d + 1, :8, :].astype(f32)], 0)
                col = (k * tiles + x) * 128
                out[:, col : col + 128] = (both * ratio).astype(bf16)

    return pl.pallas_call(
        body,
        out_shape=jax.ShapeDtypeStruct((rows, width), bf16),
        compiler_params=params(),
        name="finish",
    )(returned)


def local(gradients, second_moment, left_rows, right_root, owner_table, step_count):
    ny, nz = lax.axis_size("y"), lax.axis_size("z_hi")
    yi = lax.axis_index("y")
    group_id = lax.axis_index(REP)
    member = lax.axis_index(FS)
    members = lax.axis_size(FS)
    rows, width = gradients.shape[3], gradients.shape[4]
    blocks, size = right_root.shape[1], right_root.shape[3]
    team = members // blocks
    share = rows // team
    my_block = member // team

    gathered = lax.all_gather(left_rows[0, 0], FS, axis=0, tiled=True)
    owner_row = lax.dynamic_index_in_dim(owner_table, group_id, 0, keepdims=False)
    half = team // 2
    first = my_block * team + (member % 2) * half
    owners = lax.dynamic_slice_in_dim(owner_row, first, half, 0)
    source = (
        owners[None, :, None] * (members * share)
        + jnp.arange(members)[:, None, None] * share
        + jnp.arange(share)[None, None, :]
    ).reshape(members * half * share)
    pick = (source[:, None] == jnp.arange(members * members * share)[None, :]).astype(bf16)
    left = jnp.dot(pick, gathered, preferred_element_type=f32).astype(bf16)

    chunks = gradients.reshape(ny, nz, rows, width)
    up = [(j, (j + 1) % ny) for j in range(ny)]
    down = [(j, (j - 1) % ny) for j in range(ny)]

    def at(offset):
        return lax.rem(yi + offset + ny, ny).astype(jnp.int32).reshape(1)

    far = lax.dynamic_index_in_dim(chunks, at(4)[0], 0, keepdims=False)
    above = lax.ppermute(far[: nz // 2], "y", up)
    below = lax.ppermute(far[nz // 2 :], "y", down)
    above = ring_first(chunks, at(3), above, True)
    above = lax.ppermute(above, "y", up)
    below = ring_first(chunks, at(-3), below, False)
    below = lax.ppermute(below, "y", down)
    for s in (2, 1):
        above = lax.ppermute(ring_add(chunks, at(s), above), "y", up)
        below = lax.ppermute(ring_add(chunks, at(-s), below), "y", down)
    part = ring_add(chunks, at(0), above, below)

    parts = lax.all_to_all(part, "z_hi", 0, 0, tiled=True)
    summed, pieces = right_product(parts, right_root[0])
    columns = lax.all_to_all(pieces, FS, 0, 0, tiled=True)

    correction = 1.0 - jnp.power(f32(beta_two), step_count.astype(f32))
    new_moment, squares = adam_part(summed, second_moment[0, 0], correction, blocks)

    sent = left_product(
        left,
        columns.reshape(members * rows, 128),
        squares,
        my_block.astype(jnp.int32).reshape(1),
        members,
        blocks,
    )
    returned = lax.all_to_all(sent, FS, 0, 0, tiled=True)
    update = finish(returned, rows, width, blocks)
    return (update[None, None], new_moment[None, None])


def solution(mesh):
    fine = Mesh(mesh.devices.reshape(4, 4, 2, 8, 4), FS + REP)
    return jax.shard_map(
        local,
        mesh=fine,
        in_specs=(
            P(REP, FS, None, None, None),
            P(FS, REP, None, None),
            P(REP, FS, None, None),
            P(REP, None, None, None),
            P(),
            P(),
        ),
        out_specs=(P(FS, REP, None, None), P(FS, REP, None, None)),
        check_vma=False,
    )
```

```python
import jax
import jax.numpy as jnp
from jax import lax
from jax.experimental import pallas as pl
from jax.experimental.pallas import tpu as pltpu
from jax.sharding import Mesh, PartitionSpec as P

beta_two = 0.95
adam_eps = 1e-08
FS = ("z_lo", "x", "core")
REP = ("y", "z_hi")
f32 = jnp.float32
bf16 = jnp.bfloat16
VMEM_LIMIT = 24 * 1024 * 1024
SMEM = pl.BlockSpec(memory_space=pltpu.SMEM)
VMEM = pl.BlockSpec(memory_space=pltpu.VMEM)


def call(body, name, ins, outs, scratch=()):
    return pl.pallas_call(
        body,
        in_specs=ins,
        out_specs=jax.tree.map(lambda _: VMEM, outs),
        out_shape=outs,
        scratch_shapes=scratch,
        compiler_params=pltpu.CompilerParams(vmem_limit_bytes=VMEM_LIMIT),
        name=name,
    )


def for_sibling(chunks, index):
    _, parts, rows, width = chunks.shape

    def body(idx, own, out):
        for n in range(3):
            out[n * parts : (n + 1) * parts] = own[idx[n]]

    shape = jax.ShapeDtypeStruct((3 * parts, rows, width), bf16)
    return call(body, "for_sibling", [SMEM, VMEM], shape)(index, chunks)


def add_own(chunks, index, received):
    _, parts, rows, width = chunks.shape

    def body(idx, own, got, out):
        out[...] = (own[idx[0]].astype(f32) + got[...].astype(f32)).astype(bf16)

    shape = jax.ShapeDtypeStruct((parts, rows, width), bf16)
    return call(body, "add_own", [SMEM, VMEM, VMEM], shape)(index, chunks, received)


def add_other(others, place, received):
    parts, rows, width = received.shape

    def body(own, got, out):
        mine = own[place * parts : (place + 1) * parts]
        out[...] = (mine.astype(f32) + got[...].astype(f32)).astype(bf16)

    shape = jax.ShapeDtypeStruct((parts, rows, width), bf16)
    return call(body, "add_other", [VMEM, VMEM], shape)(others, received)


def add_last(chunks, index, one, two):
    _, parts, rows, width = chunks.shape

    def body(idx, own, a, b, *outs):
        for d in range(parts):
            p = idx[1 + d]
            total = own[idx[0], p].astype(f32) + a[p].astype(f32) + b[p].astype(f32)
            outs[d][...] = total.astype(outs[d].dtype)

    shapes = [jax.ShapeDtypeStruct((rows, width), f32 if d == 0 else bf16) for d in range(parts)]
    return call(body, "add_last", [SMEM, VMEM, VMEM, VMEM], shapes)(index, chunks, one, two)


def add_pair(one, two):
    def body(a, b, out):
        out[...] = (a[...].astype(f32) + b[...].astype(f32)).astype(bf16)

    return call(body, "add_pair", [VMEM, VMEM], jax.ShapeDtypeStruct(one.shape, bf16))(one, two)


def right_product(own, one, two, right, owners):
    rows, width = own.shape
    blocks, size, _ = right.shape
    members = owners.shape[0]
    team = members // blocks

    def body(owner, a, b, c, root, summed, pieces):
        total = a[...] + b[...].astype(f32) + c[...].astype(f32)
        summed[...] = total
        grad = total.astype(bf16)
        for k in range(blocks):
            prod = jnp.dot(
                grad[:, k * size : (k + 1) * size], root[k], preferred_element_type=f32
            ).astype(bf16)
            for i in range(team):
                pieces[owner[k * team + i]] = prod

    shapes = (
        jax.ShapeDtypeStruct((rows, width), f32),
        jax.ShapeDtypeStruct((members, rows, size), bf16),
    )
    return call(body, "right_product", [SMEM, VMEM, VMEM, VMEM, VMEM], shapes)(
        owners, own, one, two, right
    )


def adam_part(summed, moment, correction, blocks):
    rows, width = summed.shape
    size = width // blocks

    def body(corr, grad, old, new, squares):
        g = grad[...]
        m = beta_two * old[...] + (1.0 - beta_two) * g * g
        new[...] = m
        d = g / (jnp.sqrt(m / corr[0]) + adam_eps)
        d = d * d
        lane = lax.broadcasted_iota(jnp.int32, (8, 128), 1)
        acc = jnp.zeros((8, 128), f32)
        for k in range(blocks):
            acc = jnp.where(lane == k, jnp.sum(d[:, k * size : (k + 1) * size]), acc)
        squares[...] = acc

    shapes = (
        jax.ShapeDtypeStruct((rows, width), f32),
        jax.ShapeDtypeStruct((8, 128), f32),
    )
    return call(body, "adam_part", [SMEM, VMEM, VMEM], shapes)(correction, summed, moment)


def left_product(left, columns, squares, my_block, blocks):
    held, size = left.shape
    tiles = size // 128
    share = 8 // tiles
    members = held // share

    def body(block, lref, cref, sref, out):
        prod = jnp.dot(lref[...], cref[...], preferred_element_type=f32)
        lane = lax.broadcasted_iota(jnp.int32, (8, 128), 1)
        row = lax.broadcasted_iota(jnp.int32, (8, 128), 0)
        norms = jnp.where(lane == blocks + block[0], jnp.sum(prod * prod), sref[...])
        high = norms.astype(bf16).astype(f32)
        rest = norms - high
        mid = rest.astype(bf16).astype(f32)
        low = rest - mid
        tail = jnp.where(row == 0, high, jnp.where(row == 1, mid, jnp.where(row == 2, low, 0.0)))
        small = prod.astype(bf16)
        to = lax.broadcasted_iota(jnp.int32, (members * 8, held), 0)
        of = lax.broadcasted_iota(jnp.int32, (members * 8, held), 1)
        base = (of // share) * 8 + lax.rem(of, share)
        placed = jnp.zeros((members * 8, 128), f32)
        for x in range(tiles):
            pick = (to == base + x * share).astype(bf16)
            placed += jnp.dot(
                pick, small[:, x * 128 : (x + 1) * 128], preferred_element_type=f32
            )
        out[:, :8, :] = placed.reshape(members, 8, 128).astype(bf16)
        out[:, 8:, :] = jnp.broadcast_to(tail[None], (members, 8, 128)).astype(bf16)

    return call(
        body,
        "left_product",
        [SMEM, VMEM, VMEM, VMEM],
        jax.ShapeDtypeStruct((members, 16, 128), bf16),
    )(my_block, left, columns, squares)


def finish(returned, source, rows, width, blocks):
    members = returned.shape[0]
    tiles = width // blocks // 128

    def body(got, src, out):
        sums = jnp.sum(got[:, 8:, :].astype(f32), axis=0)
        sums = jnp.sum(sums, axis=0, keepdims=True)
        lane = lax.broadcasted_iota(jnp.int32, (1, 128), 1)
        count = members * 8
        ids = lax.broadcasted_iota(jnp.int32, (count, count), 1)
        pick = (src[...] == ids).astype(bf16)
        flat = got[:, :8, :].astype(f32).reshape(count, 128).astype(bf16)
        moved = jnp.dot(pick, flat, preferred_element_type=f32)
        for k in range(blocks):
            adam = jnp.sum(jnp.where(lane == k, sums, 0.0), axis=1, keepdims=True)
            shampoo = jnp.sum(jnp.where(lane == blocks + k, sums, 0.0), axis=1, keepdims=True)
            ratio = jnp.sqrt(adam / (shampoo + 1e-06))
            for x in range(tiles):
                n = k * tiles + x
                tile = moved[n * rows : (n + 1) * rows] * ratio
                out[:, n * 128 : (n + 1) * 128] = tile.astype(bf16)

    return call(body, "finish", [VMEM, VMEM], jax.ShapeDtypeStruct((rows, width), bf16))(
        returned, source
    )


def local(gradients, second_moment, left_rows, right_root, owner_table, step_count):
    ny, nz = lax.axis_size("y"), lax.axis_size("z_hi")
    yi, zi, core = lax.axis_index("y"), lax.axis_index("z_hi"), lax.axis_index("core")
    group_id = lax.axis_index(REP)
    member = lax.axis_index(FS)
    members = lax.axis_size(FS)
    rows, width = gradients.shape[3], gradients.shape[4]
    blocks, size = right_root.shape[1], right_root.shape[3]
    team = members // blocks
    share = rows // team
    tiles = size // 128
    sign = 1 - 2 * core

    def ring(n, turn):
        steps = (turn, -turn)
        return [(c * n + j, c * n + (j + steps[c]) % n) for j in range(n) for c in range(2)]

    def along_y(value):
        return lax.ppermute(value, ("core", "y"), ring(ny, 1))

    def along_z(value, turn):
        return lax.ppermute(value, ("core", "z_hi"), ring(nz, turn))

    def swap(value):
        return lax.ppermute(value, "core", [(0, 1), (1, 0)])

    def y_at(*offsets):
        return jnp.stack([jnp.bitwise_and(yi + sign * o + ny, ny - 1) for o in offsets]).astype(
            jnp.int32
        )

    chunks = gradients.reshape(ny, nz, rows, width)
    far = lax.dynamic_index_in_dim(chunks, jnp.bitwise_and(yi + 4, ny - 1), 0, keepdims=False)
    own = along_y(far)
    others = swap(for_sibling(chunks, y_at(-3, -2, -1)))
    own = along_y(add_own(chunks, y_at(3), own))
    other = along_y(others[:nz])
    own = along_y(add_own(chunks, y_at(2), own))
    other = along_y(add_other(others, 1, other))
    own = along_y(add_own(chunks, y_at(1), own))
    other = along_y(add_other(others, 2, other))
    back = swap(other)

    z_at = [jnp.bitwise_and(zi + sign * o + nz, nz - 1) for o in (0, 2, 1, -1)]
    index = jnp.stack([yi] + z_at).astype(jnp.int32)
    here, farthest, ahead, behind = add_last(chunks, index, own, back)
    farthest = along_z(farthest, 1)
    behind = along_z(behind, -1)
    ahead = along_z(add_pair(ahead, farthest), 1)

    owners = lax.dynamic_index_in_dim(owner_table, group_id, 0, keepdims=False)
    summed, pieces = right_product(here, ahead, behind, right_root[0], owners)
    columns = lax.all_to_all(pieces, FS, 0, 0, tiled=True)

    correction = 1.0 - jnp.power(f32(beta_two), step_count.astype(f32))
    new_moment, squares = adam_part(summed, second_moment[0, 0], correction, blocks)

    items = lax.broadcasted_iota(jnp.int32, (members,), 0)
    my_block = jnp.sum(jnp.where(owners == member, items // team, 0)).reshape(1)
    sent = left_product(
        left_rows[0, 0], columns.reshape(members * rows, size), squares, my_block, blocks
    )
    returned = lax.all_to_all(sent, FS, 0, 0, tiled=True)
    source = (
        owners.reshape(blocks, 1, team, 1) * 8
        + jnp.arange(tiles).reshape(1, tiles, 1, 1) * share
        + jnp.arange(share).reshape(1, 1, 1, share)
    ).reshape(members * 8, 1)
    update = finish(returned, source, rows, width, blocks)
    return (update[None, None], new_moment[None, None])


def solution(mesh):
    fine = Mesh(mesh.devices.reshape(4, 4, 2, 8, 4), FS + REP)
    return jax.shard_map(
        local,
        mesh=fine,
        in_specs=(
            P(REP, FS, None, None, None),
            P(FS, REP, None, None),
            P(REP, FS, None, None),
            P(REP, None, None, None),
            P(),
            P(),
        ),
        out_specs=(P(FS, REP, None, None), P(FS, REP, None, None)),
        check_vma=False,
    )
```

```python
import math

import jax
import jax.numpy as jnp
from jax import lax
from jax.experimental import pallas as pl
from jax.experimental.pallas import tpu as pltpu
from jax.sharding import Mesh, PartitionSpec as P

beta_two = 0.95
adam_eps = 1e-08
log_beta = math.log(beta_two)
FS = ("z_lo", "x", "core")
REP = ("y", "z_hi")
f32 = jnp.float32
bf16 = jnp.bfloat16
VMEM_LIMIT = 24 * 1024 * 1024
SMEM = pl.BlockSpec(memory_space=pltpu.SMEM)
VMEM = pl.BlockSpec(memory_space=pltpu.VMEM)


def call(body, name, ins, outs, scratch=()):
    return pl.pallas_call(
        body,
        in_specs=ins,
        out_specs=jax.tree.map(lambda _: VMEM, outs),
        out_shape=outs,
        scratch_shapes=scratch,
        compiler_params=pltpu.CompilerParams(vmem_limit_bytes=VMEM_LIMIT),
        name=name,
    )


def far_halves(chunks, index):
    _, parts, rows, width = chunks.shape
    half = parts // 2

    def body(idx, own, low, high):
        low[...] = own[0, :half]
        high[...] = own[0, half:]

    shape = jax.ShapeDtypeStruct((half, rows, width), bf16)
    block = pl.BlockSpec((half, rows, width), lambda i, idx: (0, 0, 0))
    return pl.pallas_call(
        body,
        grid_spec=pltpu.PrefetchScalarGridSpec(
            num_scalar_prefetch=1,
            grid=(1,),
            in_specs=[pl.BlockSpec((1, parts, rows, width), lambda i, idx: (idx[0], 0, 0, 0))],
            out_specs=[block, block],
        ),
        out_shape=[shape, shape],
        compiler_params=pltpu.CompilerParams(vmem_limit_bytes=VMEM_LIMIT),
        name="far_halves",
    )(index, chunks)


def ring_add(chunks, scalars, place, *received, covers=None):
    _, parts, rows, width = chunks.shape
    half = parts // 2

    def body(idx, own, *refs):
        if covers is None:
            total = own[0].astype(f32)
            for got in refs[:-1]:
                total = total + got[...].astype(f32)
            refs[-1][...] = total.astype(bf16)
        else:
            i = pl.program_id(0)

            @pl.when(i == covers)
            def _():
                refs[1][...] = (own[0].astype(f32) + refs[0][...].astype(f32)).astype(bf16)

            @pl.when(i != covers)
            def _():
                refs[1][...] = own[0]

    block = pl.BlockSpec((half, rows, width), lambda i, idx: (i, 0, 0))
    if covers is not None:
        got_block = pl.BlockSpec((half, rows, width), lambda i, idx: (0, 0, 0))
    else:
        got_block = block
    return pl.pallas_call(
        body,
        grid_spec=pltpu.PrefetchScalarGridSpec(
            num_scalar_prefetch=1,
            grid=(2,),
            in_specs=[
                pl.BlockSpec((1, half, rows, width), lambda i, idx: (idx[place], i, 0, 0))
            ]
            + [got_block] * len(received),
            out_specs=block,
        ),
        out_shape=jax.ShapeDtypeStruct((parts, rows, width), bf16),
        compiler_params=pltpu.CompilerParams(vmem_limit_bytes=VMEM_LIMIT),
        name="ring_add",
    )(scalars, chunks, *received)


def right_and_adam(parts, right, moment, scalars, step_count, owners_at, members):
    count, rows, width = parts.shape
    blocks, size, _ = right.shape
    team = members // blocks

    def body(idx, step, got, root, old, pieces, new, squares):
        total = got[0].astype(f32)
        for i in range(1, count):
            total = total + got[i].astype(f32)
        grad = total.astype(bf16)
        for k in range(blocks):
            prod = jnp.dot(
                grad[:, k * size : (k + 1) * size], root[k], preferred_element_type=f32
            ).astype(bf16)
            for i in range(team):
                pieces[idx[owners_at + k * team + i]] = prod
        steps = jnp.full((8, 128), step[0], jnp.int32).astype(f32)
        correction = (1.0 - jnp.exp(steps * log_beta))[:1, :1]
        m = beta_two * old[...] + (1.0 - beta_two) * total * total
        new[...] = m
        d = total / (jnp.sqrt(m / correction) + adam_eps)
        d = d * d
        lane = lax.broadcasted_iota(jnp.int32, (8, 128), 1)
        acc = jnp.zeros((8, 128), f32)
        for k in range(blocks):
            acc = jnp.where(lane == k, jnp.sum(d[:, k * size : (k + 1) * size]), acc)
        squares[...] = acc

    shapes = (
        jax.ShapeDtypeStruct((members, rows, size), bf16),
        jax.ShapeDtypeStruct((rows, width), f32),
        jax.ShapeDtypeStruct((8, 128), f32),
    )
    return call(body, "right_and_adam", [SMEM, SMEM, VMEM, VMEM, VMEM], shapes)(
        scalars, step_count, parts, right, moment
    )


def left_product(left, columns, squares, scalars, member_at, owners_at, blocks):
    held, size = left.shape
    tiles = size // 128
    share = 8 // tiles
    members = held // share
    team = members // blocks

    def body(idx, lref, cref, sref, out):
        prod = jnp.dot(lref[...], cref[...], preferred_element_type=f32)
        my_block = jnp.int32(0)
        for m in range(team, members):
            my_block = jnp.where(idx[owners_at + m] == idx[member_at], m // team, my_block)
        lane = lax.broadcasted_iota(jnp.int32, (8, 128), 1)
        row = lax.broadcasted_iota(jnp.int32, (8, 128), 0)
        norms = jnp.where(lane == blocks + my_block, jnp.sum(prod * prod), sref[...])
        high = norms.astype(bf16).astype(f32)
        rest = norms - high
        mid = rest.astype(bf16).astype(f32)
        low = rest - mid
        tail = jnp.where(row == 0, high, jnp.where(row == 1, mid, jnp.where(row == 2, low, 0.0)))
        small = prod.astype(bf16)
        to = lax.broadcasted_iota(jnp.int32, (members * 8, held), 0)
        of = lax.broadcasted_iota(jnp.int32, (members * 8, held), 1)
        base = (of // share) * 8 + lax.rem(of, share)
        placed = jnp.zeros((members * 8, 128), f32)
        for x in range(tiles):
            pick = (to == base + x * share).astype(bf16)
            placed += jnp.dot(
                pick, small[:, x * 128 : (x + 1) * 128], preferred_element_type=f32
            )
        out[:, :8, :] = placed.reshape(members, 8, 128).astype(bf16)
        out[:, 8:, :] = jnp.broadcast_to(tail[None], (members, 8, 128)).astype(bf16)

    return call(
        body,
        "left_product",
        [SMEM, VMEM, VMEM, VMEM],
        jax.ShapeDtypeStruct((members, 16, 128), bf16),
    )(scalars, left, columns, squares)


def finish(returned, scalars, owners_at, rows, width, blocks):
    members = returned.shape[0]
    tiles = width // blocks // 128
    team = members // blocks
    share = rows // team
    count = team * 8

    def body(idx, got, out, held):
        sums = jnp.sum(got[:, 8:, :].astype(f32), axis=0)
        sums = jnp.sum(sums, axis=0, keepdims=True)
        lane = lax.broadcasted_iota(jnp.int32, (1, 128), 1)
        to = lax.broadcasted_iota(jnp.int32, (count, count), 0)
        of = lax.broadcasted_iota(jnp.int32, (count, count), 1)
        inner = lax.rem(to, rows)
        pick = (of == (inner // share) * 8 + (to // rows) * share + lax.rem(inner, share)).astype(f32)
        for k in range(blocks):
            for i in range(team):
                m = k * team + i
                held[m] = got[idx[owners_at + m], :8, :].astype(f32)
            adam = jnp.sum(jnp.where(lane == k, sums, 0.0), axis=1, keepdims=True)
            shampoo = jnp.sum(jnp.where(lane == blocks + k, sums, 0.0), axis=1, keepdims=True)
            ratio = jnp.sqrt(adam / (shampoo + 1e-06))
            flat = held[k * team : (k + 1) * team].reshape(count, 128).astype(bf16)
            moved = jnp.dot(pick.astype(bf16), flat, preferred_element_type=f32)
            for x in range(tiles):
                n = k * tiles + x
                tile = moved[x * rows : (x + 1) * rows] * ratio
                out[:, n * 128 : (n + 1) * 128] = tile.astype(bf16)

    return call(
        body,
        "finish",
        [SMEM, VMEM],
        jax.ShapeDtypeStruct((rows, width), bf16),
        [pltpu.VMEM((members, 8, 128), f32)],
    )(scalars, returned)


def local(gradients, second_moment, left_rows, right_root, owner_table, step_count):
    ny, nz = lax.axis_size("y"), lax.axis_size("z_hi")
    yi = lax.axis_index("y")
    members = lax.axis_size(FS)
    rows, width = gradients.shape[3], gradients.shape[4]
    size = right_root.shape[3]
    blocks = right_root.shape[1]
    up = [(j, (j + 1) % ny) for j in range(ny)]
    down = [(j, (j - 1) % ny) for j in range(ny)]

    places = jnp.bitwise_and(yi + jnp.arange(ny), ny - 1)
    owners = lax.dynamic_index_in_dim(owner_table, lax.axis_index(REP), 0, keepdims=False)
    scalars = jnp.concatenate([places, lax.axis_index(FS).reshape(1), owners]).astype(jnp.int32)
    member_at, owners_at = ny, ny + 1

    chunks = gradients.reshape(ny, nz, rows, width)
    far = jnp.bitwise_and(yi + 4, ny - 1).astype(jnp.int32).reshape(1)
    above, below = far_halves(chunks, far)
    above = lax.ppermute(above, "y", up)
    below = lax.ppermute(below, "y", down)
    above = lax.ppermute(ring_add(chunks, scalars, 3, above, covers=0), "y", up)
    below = lax.ppermute(ring_add(chunks, scalars, 5, below, covers=1), "y", down)
    for s in (2, 1):
        above = lax.ppermute(ring_add(chunks, scalars, s, above), "y", up)
        below = lax.ppermute(ring_add(chunks, scalars, ny - s, below), "y", down)
    part = ring_add(chunks, scalars, 0, above, below)

    parts = lax.all_to_all(part, "z_hi", 0, 0, tiled=True)
    pieces, new_moment, squares = right_and_adam(
        parts, right_root[0], second_moment[0, 0], scalars, step_count, owners_at, members
    )
    columns = lax.all_to_all(pieces, FS, 0, 0, tiled=True).reshape(members * rows, size)
    sent = left_product(
        left_rows[0, 0], columns, squares, scalars, member_at, owners_at, blocks
    )
    returned = lax.all_to_all(sent, FS, 0, 0, tiled=True)
    update = finish(returned, scalars, owners_at, rows, width, blocks)
    return (update[None, None], new_moment[None, None])


def solution(mesh):
    fine = Mesh(mesh.devices.reshape(4, 4, 2, 8, 4), FS + REP)
    return jax.shard_map(
        local,
        mesh=fine,
        in_specs=(
            P(REP, FS, None, None, None),
            P(FS, REP, None, None),
            P(REP, FS, None, None),
            P(REP, None, None, None),
            P(),
            P(),
        ),
        out_specs=(P(FS, REP, None, None), P(FS, REP, None, None)),
        check_vma=False,
    )
```

```python
import math

import jax
import jax.numpy as jnp
from jax import lax
from jax.experimental import pallas as pl
from jax.experimental.pallas import tpu as pltpu
from jax.sharding import Mesh, PartitionSpec as P

beta_two = 0.95
adam_eps = 1e-08
log_beta = math.log(beta_two)
FS = ("z_lo", "x", "core")
REP = ("y", "z_hi")
f32 = jnp.float32
bf16 = jnp.bfloat16
VMEM_LIMIT = 24 * 1024 * 1024
SMEM = pl.BlockSpec(memory_space=pltpu.SMEM)
VMEM = pl.BlockSpec(memory_space=pltpu.VMEM)


def call(body, name, ins, outs, scratch=()):
    return pl.pallas_call(
        body,
        in_specs=ins,
        out_specs=jax.tree.map(lambda _: VMEM, outs),
        out_shape=outs,
        scratch_shapes=scratch,
        compiler_params=pltpu.CompilerParams(vmem_limit_bytes=VMEM_LIMIT),
        name=name,
    )


def take(chunks, one, two):
    _, parts, rows, width = chunks.shape

    def body(i, j, a, b, first, second):
        first[...] = a[0]
        second[...] = b[0]

    shape = jax.ShapeDtypeStruct((parts, rows, width), bf16)
    block = pl.BlockSpec((parts, rows, width), lambda g, i, j: (0, 0, 0))
    return pl.pallas_call(
        body,
        grid_spec=pltpu.PrefetchScalarGridSpec(
            num_scalar_prefetch=2,
            grid=(1,),
            in_specs=[
                pl.BlockSpec((1, parts, rows, width), lambda g, i, j: (i[0], 0, 0, 0)),
                pl.BlockSpec((1, parts, rows, width), lambda g, i, j: (j[0], 0, 0, 0)),
            ],
            out_specs=[block, block],
        ),
        out_shape=[shape, shape],
        compiler_params=pltpu.CompilerParams(vmem_limit_bytes=VMEM_LIMIT),
        name="take",
    )(one, two, chunks, chunks)


def ring_add(chunks, index, *received, after=None):
    _, parts, rows, width = chunks.shape
    half = parts // 2
    count = len(received)

    def body(idx, own, *refs):
        total = own[0].astype(f32)
        for got in refs[:count]:
            total = total + got[...].astype(f32)
        refs[-1][...] = total.astype(bf16)

    block = pl.BlockSpec((half, rows, width), lambda i, idx: (i, 0, 0))
    extra = [] if after is None else [after]
    return pl.pallas_call(
        body,
        grid_spec=pltpu.PrefetchScalarGridSpec(
            num_scalar_prefetch=1,
            grid=(2,),
            in_specs=[pl.BlockSpec((1, half, rows, width), lambda i, idx: (idx[0], i, 0, 0))]
            + [block] * count
            + [SMEM] * len(extra),
            out_specs=block,
        ),
        out_shape=jax.ShapeDtypeStruct((parts, rows, width), bf16),
        compiler_params=pltpu.CompilerParams(vmem_limit_bytes=VMEM_LIMIT),
        name="ring_add",
    )(index, chunks, *received, *extra)


def right_and_adam(parts, right, moment, scalars, step_at, owners_at, members):
    count, rows, width = parts.shape
    blocks, size, _ = right.shape
    team = members // blocks

    def body(idx, got, root, old, pieces, new, squares):
        total = got[0].astype(f32)
        for i in range(1, count):
            total = total + got[i].astype(f32)
        grad = total.astype(bf16)
        for k in range(blocks):
            prod = jnp.dot(
                grad[:, k * size : (k + 1) * size], root[k], preferred_element_type=f32
            ).astype(bf16)
            for i in range(team):
                pieces[idx[owners_at + k * team + i]] = prod
        steps = jnp.full((8, 128), idx[step_at], jnp.int32).astype(f32)
        correction = (1.0 - jnp.exp(steps * log_beta))[:1, :1]
        m = beta_two * old[...] + (1.0 - beta_two) * total * total
        new[...] = m
        d = total / (jnp.sqrt(m / correction) + adam_eps)
        d = d * d
        lane = lax.broadcasted_iota(jnp.int32, (8, 128), 1)
        acc = jnp.zeros((8, 128), f32)
        for k in range(blocks):
            acc = jnp.where(lane == k, jnp.sum(d[:, k * size : (k + 1) * size]), acc)
        squares[...] = acc

    shapes = (
        jax.ShapeDtypeStruct((members, rows, size), bf16),
        jax.ShapeDtypeStruct((rows, width), f32),
        jax.ShapeDtypeStruct((8, 128), f32),
    )
    return call(body, "right_and_adam", [SMEM, VMEM, VMEM, VMEM], shapes)(
        scalars, parts, right, moment
    )


def left_product(left, columns, squares, scalars, member_at, owners_at, blocks):
    held, size = left.shape
    tiles = size // 128
    share = 8 // tiles
    members = held // share
    team = members // blocks

    def body(idx, lref, cref, sref, out):
        prod = jnp.dot(lref[...], cref[...], preferred_element_type=f32)
        my_block = jnp.int32(0)
        for m in range(team, members):
            my_block = jnp.where(idx[owners_at + m] == idx[member_at], m // team, my_block)
        lane = lax.broadcasted_iota(jnp.int32, (8, 128), 1)
        row = lax.broadcasted_iota(jnp.int32, (8, 128), 0)
        norms = jnp.where(lane == blocks + my_block, jnp.sum(prod * prod), sref[...])
        high = norms.astype(bf16).astype(f32)
        rest = norms - high
        mid = rest.astype(bf16).astype(f32)
        low = rest - mid
        tail = jnp.where(row == 0, high, jnp.where(row == 1, mid, jnp.where(row == 2, low, 0.0)))
        small = prod.astype(bf16)
        to = lax.broadcasted_iota(jnp.int32, (members * 8, held), 0)
        of = lax.broadcasted_iota(jnp.int32, (members * 8, held), 1)
        base = (of // share) * 8 + lax.rem(of, share)
        placed = jnp.zeros((members * 8, 128), f32)
        for x in range(tiles):
            pick = (to == base + x * share).astype(bf16)
            placed += jnp.dot(
                pick, small[:, x * 128 : (x + 1) * 128], preferred_element_type=f32
            )
        out[:, :8, :] = placed.reshape(members, 8, 128).astype(bf16)
        out[:, 8:, :] = jnp.broadcast_to(tail[None], (members, 8, 128)).astype(bf16)

    return call(
        body,
        "left_product",
        [SMEM, VMEM, VMEM, VMEM],
        jax.ShapeDtypeStruct((members, 16, 128), bf16),
    )(scalars, left, columns, squares)


def finish(returned, scalars, owners_at, rows, width, blocks):
    members = returned.shape[0]
    tiles = width // blocks // 128
    team = members // blocks
    share = rows // team
    count = team * 8

    def body(idx, got, out, held):
        sums = jnp.sum(got[:, 8:, :].astype(f32), axis=0)
        sums = jnp.sum(sums, axis=0, keepdims=True)
        lane = lax.broadcasted_iota(jnp.int32, (1, 128), 1)
        to = lax.broadcasted_iota(jnp.int32, (count, count), 0)
        of = lax.broadcasted_iota(jnp.int32, (count, count), 1)
        inner = lax.rem(to, rows)
        pick = (of == (inner // share) * 8 + (to // rows) * share + lax.rem(inner, share)).astype(f32)
        for k in range(blocks):
            for i in range(team):
                m = k * team + i
                held[m] = got[idx[owners_at + m], :8, :].astype(f32)
            adam = jnp.sum(jnp.where(lane == k, sums, 0.0), axis=1, keepdims=True)
            shampoo = jnp.sum(jnp.where(lane == blocks + k, sums, 0.0), axis=1, keepdims=True)
            ratio = jnp.sqrt(adam / (shampoo + 1e-06))
            flat = held[k * team : (k + 1) * team].reshape(count, 128).astype(bf16)
            moved = jnp.dot(pick.astype(bf16), flat, preferred_element_type=f32)
            for x in range(tiles):
                n = k * tiles + x
                tile = moved[x * rows : (x + 1) * rows] * ratio
                out[:, n * 128 : (n + 1) * 128] = tile.astype(bf16)

    return call(
        body,
        "finish",
        [SMEM, VMEM],
        jax.ShapeDtypeStruct((rows, width), bf16),
        [pltpu.VMEM((members, 8, 128), f32)],
    )(scalars, returned)


def local(gradients, second_moment, left_rows, right_root, owner_table, step_count):
    ny, nz = lax.axis_size("y"), lax.axis_size("z_hi")
    yi = lax.axis_index("y")
    members = lax.axis_size(FS)
    rows, width = gradients.shape[3], gradients.shape[4]
    size = right_root.shape[3]
    blocks = right_root.shape[1]
    sign = 1 - 2 * lax.axis_index("core")

    def along(value, turn):
        steps = (turn, -turn)
        pairs = [(c * ny + j, c * ny + (j + steps[c]) % ny) for c in range(2) for j in range(ny)]
        return lax.ppermute(value, ("core", "y"), pairs)

    def at(offset):
        return jnp.bitwise_and(yi + sign * offset + ny, ny - 1).astype(jnp.int32).reshape(1)

    owners = lax.dynamic_index_in_dim(owner_table, lax.axis_index(REP), 0, keepdims=False)
    scalars = jnp.concatenate([lax.axis_index(FS).reshape(1), step_count, owners]).astype(jnp.int32)
    member_at, step_at, owners_at = 0, 1, 2

    chunks = gradients.reshape(ny, nz, rows, width)
    long_way, short_way = take(chunks, at(4), at(-3))
    long_way = along(long_way, 1)
    short_way = along(short_way, -1)
    long_way = along(ring_add(chunks, at(3), long_way, after=scalars), 1)
    short_way = along(ring_add(chunks, at(-2), short_way), -1)
    long_way = along(ring_add(chunks, at(2), long_way), 1)
    short_way = along(ring_add(chunks, at(-1), short_way), -1)
    long_way = along(ring_add(chunks, at(1), long_way), 1)
    part = ring_add(chunks, at(0), long_way, short_way)

    parts = lax.all_to_all(part, "z_hi", 0, 0, tiled=True)
    pieces, new_moment, squares = right_and_adam(
        parts, right_root[0], second_moment[0, 0], scalars, step_at, owners_at, members
    )
    columns = lax.all_to_all(pieces, FS, 0, 0, tiled=True).reshape(members * rows, size)
    sent = left_product(
        left_rows[0, 0], columns, squares, scalars, member_at, owners_at, blocks
    )
    returned = lax.all_to_all(sent, FS, 0, 0, tiled=True)
    update = finish(returned, scalars, owners_at, rows, width, blocks)
    return (update[None, None], new_moment[None, None])


def solution(mesh):
    fine = Mesh(mesh.devices.reshape(4, 4, 2, 8, 4), FS + REP)
    return jax.shard_map(
        local,
        mesh=fine,
        in_specs=(
            P(REP, FS, None, None, None),
            P(FS, REP, None, None),
            P(REP, FS, None, None),
            P(REP, None, None, None),
            P(),
            P(),
        ),
        out_specs=(P(FS, REP, None, None), P(FS, REP, None, None)),
        check_vma=False,
    )
```

```python
import math

import jax
import jax.numpy as jnp
from jax import lax
from jax.experimental import pallas as pl
from jax.experimental.pallas import tpu as pltpu
from jax.sharding import Mesh, PartitionSpec as P

beta_two = 0.95
adam_eps = 1e-08
log_beta = math.log(beta_two)
FS = ("z_lo", "x", "core")
REP = ("y", "z_hi")
f32 = jnp.float32
bf16 = jnp.bfloat16
VMEM_LIMIT = 24 * 1024 * 1024
SMEM = pl.BlockSpec(memory_space=pltpu.SMEM)
VMEM = pl.BlockSpec(memory_space=pltpu.VMEM)


def call(body, name, ins, outs, scratch=()):
    return pl.pallas_call(
        body,
        in_specs=ins,
        out_specs=jax.tree.map(lambda _: VMEM, outs),
        out_shape=outs,
        scratch_shapes=scratch,
        compiler_params=pltpu.CompilerParams(vmem_limit_bytes=VMEM_LIMIT),
        name=name,
    )


def take(chunks, *places):
    _, parts, rows, width = chunks.shape
    count = len(places)

    def body(*refs):
        ins, outs = refs[count : 2 * count], refs[2 * count :]
        for got, out in zip(ins, outs):
            out[...] = got[0]

    def block_at(n):
        return pl.BlockSpec((1, parts, rows, width), lambda g, *idx: (idx[n][0], 0, 0, 0))

    shape = jax.ShapeDtypeStruct((parts, rows, width), bf16)
    return pl.pallas_call(
        body,
        grid_spec=pltpu.PrefetchScalarGridSpec(
            num_scalar_prefetch=count,
            grid=(1,),
            in_specs=[block_at(n) for n in range(count)],
            out_specs=[pl.BlockSpec((parts, rows, width), lambda g, *idx: (0, 0, 0))] * count,
        ),
        out_shape=[shape] * count,
        compiler_params=pltpu.CompilerParams(vmem_limit_bytes=VMEM_LIMIT),
        name="take",
    )(*places, *[chunks] * count)


def ring_add(chunks, index, *received, also=None, after=None):
    _, parts, rows, width = chunks.shape
    half = parts // 2
    count = len(received)
    places = [index] + ([] if also is None else [also])
    wanted = len(places)

    def body(*refs):
        own = refs[wanted : 2 * wanted]
        outs = refs[-wanted:]
        total = own[0][0].astype(f32)
        for got in refs[2 * wanted : 2 * wanted + count]:
            total = total + got[...].astype(f32)
        outs[0][...] = total.astype(bf16)
        if wanted == 2:
            outs[1][...] = own[1][0]

    def block_at(n):
        return pl.BlockSpec((1, half, rows, width), lambda i, *idx: (idx[n][0], i, 0, 0))

    block = pl.BlockSpec((half, rows, width), lambda i, *idx: (i, 0, 0))
    extra = [] if after is None else [after]
    out = pl.pallas_call(
        body,
        grid_spec=pltpu.PrefetchScalarGridSpec(
            num_scalar_prefetch=wanted,
            grid=(2,),
            in_specs=[block_at(n) for n in range(wanted)] + [block] * count + [SMEM] * len(extra),
            out_specs=[block] * wanted,
        ),
        out_shape=[jax.ShapeDtypeStruct((parts, rows, width), bf16)] * wanted,
        compiler_params=pltpu.CompilerParams(vmem_limit_bytes=VMEM_LIMIT),
        name="ring_add",
    )(*places, *[chunks] * wanted, *received, *extra)
    return out[0] if also is None else out


def right_and_adam(parts, right, moment, scalars, step_at, owners_at, members):
    count, rows, width = parts.shape
    blocks, size, _ = right.shape
    team = members // blocks

    def body(idx, got, root, old, pieces, new, squares):
        total = got[0].astype(f32)
        for i in range(1, count):
            total = total + got[i].astype(f32)
        grad = total.astype(bf16)
        for k in range(blocks):
            prod = jnp.dot(
                grad[:, k * size : (k + 1) * size], root[k], preferred_element_type=f32
            ).astype(bf16)
            for i in range(team):
                pieces[idx[owners_at + k * team + i]] = prod
        steps = jnp.full((8, 128), idx[step_at], jnp.int32).astype(f32)
        correction = (1.0 - jnp.exp(steps * log_beta))[:1, :1]
        m = beta_two * old[...] + (1.0 - beta_two) * total * total
        new[...] = m
        d = total / (jnp.sqrt(m / correction) + adam_eps)
        d = d * d
        lane = lax.broadcasted_iota(jnp.int32, (8, 128), 1)
        acc = jnp.zeros((8, 128), f32)
        for k in range(blocks):
            acc = jnp.where(lane == k, jnp.sum(d[:, k * size : (k + 1) * size]), acc)
        squares[...] = acc

    shapes = (
        jax.ShapeDtypeStruct((members, rows, size), bf16),
        jax.ShapeDtypeStruct((rows, width), f32),
        jax.ShapeDtypeStruct((8, 128), f32),
    )
    return call(body, "right_and_adam", [SMEM, VMEM, VMEM, VMEM], shapes)(
        scalars, parts, right, moment
    )


def left_product(left, columns, squares, scalars, member_at, owners_at, blocks):
    held, size = left.shape
    tiles = size // 128
    share = 8 // tiles
    members = held // share
    team = members // blocks

    def body(idx, lref, cref, sref, out):
        prod = jnp.dot(lref[...], cref[...], preferred_element_type=f32)
        my_block = jnp.int32(0)
        for m in range(team, members):
            my_block = jnp.where(idx[owners_at + m] == idx[member_at], m // team, my_block)
        lane = lax.broadcasted_iota(jnp.int32, (8, 128), 1)
        row = lax.broadcasted_iota(jnp.int32, (8, 128), 0)
        norms = jnp.where(lane == blocks + my_block, jnp.sum(prod * prod), sref[...])
        high = norms.astype(bf16).astype(f32)
        rest = norms - high
        mid = rest.astype(bf16).astype(f32)
        low = rest - mid
        tail = jnp.where(row == 0, high, jnp.where(row == 1, mid, jnp.where(row == 2, low, 0.0)))
        small = prod.astype(bf16)
        to = lax.broadcasted_iota(jnp.int32, (members * 8, held), 0)
        of = lax.broadcasted_iota(jnp.int32, (members * 8, held), 1)
        base = (of // share) * 8 + lax.rem(of, share)
        placed = jnp.zeros((members * 8, 128), f32)
        for x in range(tiles):
            pick = (to == base + x * share).astype(bf16)
            placed += jnp.dot(
                pick, small[:, x * 128 : (x + 1) * 128], preferred_element_type=f32
            )
        out[:, :8, :] = placed.reshape(members, 8, 128).astype(bf16)
        out[:, 8:, :] = jnp.broadcast_to(tail[None], (members, 8, 128)).astype(bf16)

    return call(
        body,
        "left_product",
        [SMEM, VMEM, VMEM, VMEM],
        jax.ShapeDtypeStruct((members, 16, 128), bf16),
    )(scalars, left, columns, squares)


def finish(returned, scalars, owners_at, rows, width, blocks):
    members = returned.shape[0]
    tiles = width // blocks // 128
    team = members // blocks
    share = rows // team
    count = team * 8

    def body(idx, got, out, held):
        sums = jnp.sum(got[:, 8:, :].astype(f32), axis=0)
        sums = jnp.sum(sums, axis=0, keepdims=True)
        lane = lax.broadcasted_iota(jnp.int32, (1, 128), 1)
        to = lax.broadcasted_iota(jnp.int32, (count, count), 0)
        of = lax.broadcasted_iota(jnp.int32, (count, count), 1)
        inner = lax.rem(to, rows)
        pick = (of == (inner // share) * 8 + (to // rows) * share + lax.rem(inner, share)).astype(f32)
        for k in range(blocks):
            for i in range(team):
                m = k * team + i
                held[m] = got[idx[owners_at + m], :8, :].astype(f32)
            adam = jnp.sum(jnp.where(lane == k, sums, 0.0), axis=1, keepdims=True)
            shampoo = jnp.sum(jnp.where(lane == blocks + k, sums, 0.0), axis=1, keepdims=True)
            ratio = jnp.sqrt(adam / (shampoo + 1e-06))
            flat = held[k * team : (k + 1) * team].reshape(count, 128).astype(bf16)
            moved = jnp.dot(pick.astype(bf16), flat, preferred_element_type=f32)
            for x in range(tiles):
                n = k * tiles + x
                tile = moved[x * rows : (x + 1) * rows] * ratio
                out[:, n * 128 : (n + 1) * 128] = tile.astype(bf16)

    return call(
        body,
        "finish",
        [SMEM, VMEM],
        jax.ShapeDtypeStruct((rows, width), bf16),
        [pltpu.VMEM((members, 8, 128), f32)],
    )(scalars, returned)


def local(gradients, second_moment, left_rows, right_root, owner_table, step_count):
    ny, nz = lax.axis_size("y"), lax.axis_size("z_hi")
    yi = lax.axis_index("y")
    members = lax.axis_size(FS)
    rows, width = gradients.shape[3], gradients.shape[4]
    size = right_root.shape[3]
    blocks = right_root.shape[1]
    sign = 1 - 2 * lax.axis_index("core")

    def along(value, turn):
        steps = (turn, -turn)
        pairs = [(c * ny + j, c * ny + (j + steps[c]) % ny) for c in range(2) for j in range(ny)]
        return lax.ppermute(value, ("core", "y"), pairs)

    def at(offset):
        return jnp.bitwise_and(yi + sign * offset + ny, ny - 1).astype(jnp.int32).reshape(1)

    owners = lax.dynamic_index_in_dim(owner_table, lax.axis_index(REP), 0, keepdims=False)
    scalars = jnp.concatenate([lax.axis_index(FS).reshape(1), step_count, owners]).astype(jnp.int32)
    member_at, step_at, owners_at = 0, 1, 2

    chunks = gradients.reshape(ny, nz, rows, width)
    four = along(lax.dynamic_index_in_dim(chunks, at(4)[0], 0, keepdims=False), 1)
    minus_two, two = take(chunks, at(-2), at(2))
    minus_two = along(minus_two, -1)
    two = along(two, 1)
    three = along(ring_add(chunks, at(3), four), 2)
    minus_one, minus_three = ring_add(chunks, at(-1), minus_two, also=at(-3), after=scalars)
    minus_one = along(minus_one, -1)
    minus_three = along(minus_three, -3)
    one = along(ring_add(chunks, at(1), two, three), 1)
    part = ring_add(chunks, at(0), minus_one, minus_three, one)

    parts = lax.all_to_all(part, "z_hi", 0, 0, tiled=True)
    pieces, new_moment, squares = right_and_adam(
        parts, right_root[0], second_moment[0, 0], scalars, step_at, owners_at, members
    )
    columns = lax.all_to_all(pieces, FS, 0, 0, tiled=True).reshape(members * rows, size)
    sent = left_product(
        left_rows[0, 0], columns, squares, scalars, member_at, owners_at, blocks
    )
    returned = lax.all_to_all(sent, FS, 0, 0, tiled=True)
    update = finish(returned, scalars, owners_at, rows, width, blocks)
    return (update[None, None], new_moment[None, None])


def solution(mesh):
    fine = Mesh(mesh.devices.reshape(4, 4, 2, 8, 4), FS + REP)
    return jax.shard_map(
        local,
        mesh=fine,
        in_specs=(
            P(REP, FS, None, None, None),
            P(FS, REP, None, None),
            P(REP, FS, None, None),
            P(REP, None, None, None),
            P(),
            P(),
        ),
        out_specs=(P(FS, REP, None, None), P(FS, REP, None, None)),
        check_vma=False,
    )
```

```python
import math

import jax
import jax.numpy as jnp
from jax import lax
from jax.experimental import pallas as pl
from jax.experimental.pallas import tpu as pltpu
from jax.sharding import Mesh, PartitionSpec as P

beta_two = 0.95
adam_eps = 1e-08
log_beta = math.log(beta_two)
FS = ("z_lo", "x", "core")
REP = ("y", "z_hi")
f32 = jnp.float32
bf16 = jnp.bfloat16
VMEM_LIMIT = 24 * 1024 * 1024
SMEM = pl.BlockSpec(memory_space=pltpu.SMEM)
VMEM = pl.BlockSpec(memory_space=pltpu.VMEM)


def call(body, name, ins, outs, scratch=()):
    return pl.pallas_call(
        body,
        in_specs=ins,
        out_specs=jax.tree.map(lambda _: VMEM, outs),
        out_shape=outs,
        scratch_shapes=scratch,
        compiler_params=pltpu.CompilerParams(vmem_limit_bytes=VMEM_LIMIT),
        name=name,
    )


def take(chunks, *places):
    _, parts, rows, width = chunks.shape
    count = len(places)

    def body(*refs):
        ins, outs = refs[count : 2 * count], refs[2 * count :]
        for got, out in zip(ins, outs):
            out[...] = got[0]

    def block_at(n):
        return pl.BlockSpec((1, parts, rows, width), lambda g, *idx: (idx[n][0], 0, 0, 0))

    shape = jax.ShapeDtypeStruct((parts, rows, width), bf16)
    return pl.pallas_call(
        body,
        grid_spec=pltpu.PrefetchScalarGridSpec(
            num_scalar_prefetch=count,
            grid=(1,),
            in_specs=[block_at(n) for n in range(count)],
            out_specs=[pl.BlockSpec((parts, rows, width), lambda g, *idx: (0, 0, 0))] * count,
        ),
        out_shape=[shape] * count,
        compiler_params=pltpu.CompilerParams(vmem_limit_bytes=VMEM_LIMIT),
        name="take",
    )(*places, *[chunks] * count)


def ring_add(chunks, index, *received, also=None, after=None):
    _, parts, rows, width = chunks.shape
    half = parts // 2
    count = len(received)
    places = [index] + ([] if also is None else [also])
    wanted = len(places)

    def body(*refs):
        own = refs[wanted : 2 * wanted]
        outs = refs[-wanted:]
        total = own[0][0].astype(f32)
        for got in refs[2 * wanted : 2 * wanted + count]:
            total = total + got[...].astype(f32)
        outs[0][...] = total.astype(bf16)
        if wanted == 2:
            outs[1][...] = own[1][0]

    def block_at(n):
        return pl.BlockSpec((1, half, rows, width), lambda i, *idx: (idx[n][0], i, 0, 0))

    block = pl.BlockSpec((half, rows, width), lambda i, *idx: (i, 0, 0))
    extra = [] if after is None else [after]
    out = pl.pallas_call(
        body,
        grid_spec=pltpu.PrefetchScalarGridSpec(
            num_scalar_prefetch=wanted,
            grid=(2,),
            in_specs=[block_at(n) for n in range(wanted)] + [block] * count + [SMEM] * len(extra),
            out_specs=[block] * wanted,
        ),
        out_shape=[jax.ShapeDtypeStruct((parts, rows, width), bf16)] * wanted,
        compiler_params=pltpu.CompilerParams(vmem_limit_bytes=VMEM_LIMIT),
        name="ring_add",
    )(*places, *[chunks] * wanted, *received, *extra)
    return out[0] if also is None else out


def right_and_adam(parts, right, moment, scalars, step_at, owners_at, members):
    count, rows, width = parts.shape
    blocks, size, _ = right.shape
    team = members // blocks

    def body(idx, got, root, old, pieces, new, squares):
        total = got[0].astype(f32)
        for i in range(1, count):
            total = total + got[i].astype(f32)
        grad = total.astype(bf16)
        for k in range(blocks):
            prod = jnp.dot(
                grad[:, k * size : (k + 1) * size], root[k], preferred_element_type=f32
            ).astype(bf16)
            for i in range(team):
                pieces[idx[owners_at + k * team + i]] = prod
        steps = jnp.full((8, 128), idx[step_at], jnp.int32).astype(f32)
        correction = (1.0 - jnp.exp(steps * log_beta))[:1, :1]
        m = beta_two * old[...] + (1.0 - beta_two) * total * total
        new[...] = m
        d = total / (jnp.sqrt(m / correction) + adam_eps)
        d = d * d
        lane = lax.broadcasted_iota(jnp.int32, (8, 128), 1)
        acc = jnp.zeros((8, 128), f32)
        for k in range(blocks):
            acc = jnp.where(lane == k, jnp.sum(d[:, k * size : (k + 1) * size]), acc)
        squares[...] = acc

    shapes = (
        jax.ShapeDtypeStruct((members, rows, size), bf16),
        jax.ShapeDtypeStruct((rows, width), f32),
        jax.ShapeDtypeStruct((8, 128), f32),
    )
    return call(body, "right_and_adam", [SMEM, VMEM, VMEM, VMEM], shapes)(
        scalars, parts, right, moment
    )


def left_product(left, columns, squares, scalars, member_at, owners_at, blocks):
    held, size = left.shape
    tiles = size // 128
    share = 8 // tiles
    members = held // share
    team = members // blocks

    def body(idx, lref, cref, sref, out):
        prod = jnp.dot(lref[...], cref[...], preferred_element_type=f32)
        my_block = jnp.int32(0)
        for m in range(team, members):
            my_block = jnp.where(idx[owners_at + m] == idx[member_at], m // team, my_block)
        lane = lax.broadcasted_iota(jnp.int32, (8, 128), 1)
        row = lax.broadcasted_iota(jnp.int32, (8, 128), 0)
        norms = jnp.where(lane == blocks + my_block, jnp.sum(prod * prod), sref[...])
        high = norms.astype(bf16).astype(f32)
        rest = norms - high
        mid = rest.astype(bf16).astype(f32)
        low = rest - mid
        tail = jnp.where(row == 0, high, jnp.where(row == 1, mid, jnp.where(row == 2, low, 0.0)))
        small = prod.astype(bf16)
        to = lax.broadcasted_iota(jnp.int32, (members * 8, held), 0)
        of = lax.broadcasted_iota(jnp.int32, (members * 8, held), 1)
        base = (of // share) * 8 + lax.rem(of, share)
        placed = jnp.zeros((members * 8, 128), f32)
        for x in range(tiles):
            pick = (to == base + x * share).astype(bf16)
            placed += jnp.dot(
                pick, small[:, x * 128 : (x + 1) * 128], preferred_element_type=f32
            )
        out[:, :8, :] = placed.reshape(members, 8, 128).astype(bf16)
        out[:, 8:, :] = jnp.broadcast_to(tail[None], (members, 8, 128)).astype(bf16)

    return call(
        body,
        "left_product",
        [SMEM, VMEM, VMEM, VMEM],
        jax.ShapeDtypeStruct((members, 16, 128), bf16),
    )(scalars, left, columns, squares)


def finish(returned, scalars, owners_at, rows, width, blocks):
    members = returned.shape[0]
    tiles = width // blocks // 128
    team = members // blocks
    share = rows // team
    count = team * 8

    def body(idx, got, out, held):
        sums = jnp.sum(got[:, 8:, :].astype(f32), axis=0)
        sums = jnp.sum(sums, axis=0, keepdims=True)
        lane = lax.broadcasted_iota(jnp.int32, (1, 128), 1)
        to = lax.broadcasted_iota(jnp.int32, (count, count), 0)
        of = lax.broadcasted_iota(jnp.int32, (count, count), 1)
        inner = lax.rem(to, rows)
        pick = (of == (inner // share) * 8 + (to // rows) * share + lax.rem(inner, share)).astype(f32)
        for k in range(blocks):
            for i in range(team):
                m = k * team + i
                held[m] = got[idx[owners_at + m], :8, :].astype(f32)
            adam = jnp.sum(jnp.where(lane == k, sums, 0.0), axis=1, keepdims=True)
            shampoo = jnp.sum(jnp.where(lane == blocks + k, sums, 0.0), axis=1, keepdims=True)
            ratio = jnp.sqrt(adam / (shampoo + 1e-06))
            flat = held[k * team : (k + 1) * team].reshape(count, 128).astype(bf16)
            moved = jnp.dot(pick.astype(bf16), flat, preferred_element_type=f32)
            for x in range(tiles):
                n = k * tiles + x
                tile = moved[x * rows : (x + 1) * rows] * ratio
                out[:, n * 128 : (n + 1) * 128] = tile.astype(bf16)

    return call(
        body,
        "finish",
        [SMEM, VMEM],
        jax.ShapeDtypeStruct((rows, width), bf16),
        [pltpu.VMEM((members, 8, 128), f32)],
    )(scalars, returned)


def local(gradients, second_moment, left_rows, right_root, owner_table, step_count):
    ny, nz = lax.axis_size("y"), lax.axis_size("z_hi")
    yi = lax.axis_index("y")
    members = lax.axis_size(FS)
    rows, width = gradients.shape[3], gradients.shape[4]
    size = right_root.shape[3]
    blocks = right_root.shape[1]
    sign = 1 - 2 * lax.axis_index("core")

    def along(value, turn):
        steps = (turn, -turn)
        pairs = [(c * ny + j, c * ny + (j + steps[c]) % ny) for c in range(2) for j in range(ny)]
        return lax.ppermute(value, ("core", "y"), pairs)

    def at(offset):
        return jnp.bitwise_and(yi + sign * offset + ny, ny - 1).astype(jnp.int32).reshape(1)

    owners = lax.dynamic_index_in_dim(owner_table, lax.axis_index(REP), 0, keepdims=False)
    scalars = jnp.concatenate([lax.axis_index(FS).reshape(1), step_count, owners]).astype(jnp.int32)
    member_at, step_at, owners_at = 0, 1, 2

    chunks = gradients.reshape(ny, nz, rows, width)
    four = along(lax.dynamic_index_in_dim(chunks, at(4)[0], 0, keepdims=False), 1)
    minus_three, two = take(chunks, at(-3), at(2))
    minus_three = along(minus_three, -2)
    two = along(two, 1)
    three, minus_two = ring_add(chunks, at(3), four, also=at(-2))
    three = along(three, 2)
    minus_two = along(minus_two, -1)
    minus_one = along(ring_add(chunks, at(-1), minus_two, minus_three), -1)
    one = along(ring_add(chunks, at(1), two, three), 1)
    part = ring_add(chunks, at(0), minus_one, one, after=scalars)

    parts = lax.all_to_all(part, "z_hi", 0, 0, tiled=True)
    pieces, new_moment, squares = right_and_adam(
        parts, right_root[0], second_moment[0, 0], scalars, step_at, owners_at, members
    )
    columns = lax.all_to_all(pieces, FS, 0, 0, tiled=True).reshape(members * rows, size)
    sent = left_product(
        left_rows[0, 0], columns, squares, scalars, member_at, owners_at, blocks
    )
    returned = lax.all_to_all(sent, FS, 0, 0, tiled=True)
    update = finish(returned, scalars, owners_at, rows, width, blocks)
    return (update[None, None], new_moment[None, None])


def solution(mesh):
    fine = Mesh(mesh.devices.reshape(4, 4, 2, 8, 4), FS + REP)
    return jax.shard_map(
        local,
        mesh=fine,
        in_specs=(
            P(REP, FS, None, None, None),
            P(FS, REP, None, None),
            P(REP, FS, None, None),
            P(REP, None, None, None),
            P(),
            P(),
        ),
        out_specs=(P(FS, REP, None, None), P(FS, REP, None, None)),
        check_vma=False,
    )
```

```python
import math

import jax
import jax.numpy as jnp
from jax import lax
from jax.experimental import pallas as pl
from jax.experimental.pallas import tpu as pltpu
from jax.sharding import Mesh, PartitionSpec as P

beta_two = 0.95
adam_eps = 1e-08
log_beta = math.log(beta_two)
FS = ("z_lo", "x", "core")
REP = ("y", "z_hi")
f32 = jnp.float32
bf16 = jnp.bfloat16
VMEM_LIMIT = 24 * 1024 * 1024
SMEM = pl.BlockSpec(memory_space=pltpu.SMEM)
VMEM = pl.BlockSpec(memory_space=pltpu.VMEM)


def call(body, name, ins, outs, scratch=()):
    return pl.pallas_call(
        body,
        in_specs=ins,
        out_specs=jax.tree.map(lambda _: VMEM, outs),
        out_shape=outs,
        scratch_shapes=scratch,
        compiler_params=pltpu.CompilerParams(vmem_limit_bytes=VMEM_LIMIT),
        name=name,
    )


def take(chunks, *places):
    _, parts, rows, width = chunks.shape
    count = len(places)

    def body(*refs):
        ins, outs = refs[count : 2 * count], refs[2 * count :]
        for got, out in zip(ins, outs):
            out[...] = got[0]

    def block_at(n):
        return pl.BlockSpec((1, parts, rows, width), lambda g, *idx: (idx[n][0], 0, 0, 0))

    shape = jax.ShapeDtypeStruct((parts, rows, width), bf16)
    return pl.pallas_call(
        body,
        grid_spec=pltpu.PrefetchScalarGridSpec(
            num_scalar_prefetch=count,
            grid=(1,),
            in_specs=[block_at(n) for n in range(count)],
            out_specs=[pl.BlockSpec((parts, rows, width), lambda g, *idx: (0, 0, 0))] * count,
        ),
        out_shape=[shape] * count,
        compiler_params=pltpu.CompilerParams(vmem_limit_bytes=VMEM_LIMIT),
        name="take",
    )(*places, *[chunks] * count)


def ring_add(chunks, index, *received, also=(), after=None):
    _, parts, rows, width = chunks.shape
    half = parts // 2
    count = len(received)
    places = [index, *also]
    wanted = len(places)

    def body(*refs):
        own = refs[wanted : 2 * wanted]
        outs = refs[-wanted:]
        total = own[0][0].astype(f32)
        for got in refs[2 * wanted : 2 * wanted + count]:
            total = total + got[...].astype(f32)
        outs[0][...] = total.astype(bf16)
        for copied, out in zip(own[1:], outs[1:]):
            out[...] = copied[0]

    def block_at(n):
        return pl.BlockSpec((1, half, rows, width), lambda i, *idx: (idx[n][0], i, 0, 0))

    block = pl.BlockSpec((half, rows, width), lambda i, *idx: (i, 0, 0))
    extra = [] if after is None else [after]
    out = pl.pallas_call(
        body,
        grid_spec=pltpu.PrefetchScalarGridSpec(
            num_scalar_prefetch=wanted,
            grid=(2,),
            in_specs=[block_at(n) for n in range(wanted)] + [block] * count + [SMEM] * len(extra),
            out_specs=[block] * wanted,
        ),
        out_shape=[jax.ShapeDtypeStruct((parts, rows, width), bf16)] * wanted,
        compiler_params=pltpu.CompilerParams(vmem_limit_bytes=VMEM_LIMIT),
        name="ring_add",
    )(*places, *[chunks] * wanted, *received, *extra)
    return out if also else out[0]


def right_and_adam(parts, right, moment, scalars, step_at, owners_at, members):
    count, rows, width = parts.shape
    blocks, size, _ = right.shape
    team = members // blocks

    def body(idx, got, root, old, pieces, new, squares):
        total = got[0].astype(f32)
        for i in range(1, count):
            total = total + got[i].astype(f32)
        grad = total.astype(bf16)
        for k in range(blocks):
            prod = jnp.dot(
                grad[:, k * size : (k + 1) * size], root[k], preferred_element_type=f32
            ).astype(bf16)
            for i in range(team):
                pieces[idx[owners_at + k * team + i]] = prod
        steps = jnp.full((8, 128), idx[step_at], jnp.int32).astype(f32)
        correction = (1.0 - jnp.exp(steps * log_beta))[:1, :1]
        m = beta_two * old[...] + (1.0 - beta_two) * total * total
        new[...] = m
        d = total / (jnp.sqrt(m / correction) + adam_eps)
        d = d * d
        lane = lax.broadcasted_iota(jnp.int32, (8, 128), 1)
        acc = jnp.zeros((8, 128), f32)
        for k in range(blocks):
            acc = jnp.where(lane == k, jnp.sum(d[:, k * size : (k + 1) * size]), acc)
        squares[...] = acc

    shapes = (
        jax.ShapeDtypeStruct((members, rows, size), bf16),
        jax.ShapeDtypeStruct((rows, width), f32),
        jax.ShapeDtypeStruct((8, 128), f32),
    )
    return call(body, "right_and_adam", [SMEM, VMEM, VMEM, VMEM], shapes)(
        scalars, parts, right, moment
    )


def left_product(left, columns, squares, scalars, member_at, owners_at, blocks):
    held, size = left.shape
    tiles = size // 128
    share = 8 // tiles
    members = held // share
    team = members // blocks

    def body(idx, lref, cref, sref, out):
        prod = jnp.dot(lref[...], cref[...], preferred_element_type=f32)
        my_block = jnp.int32(0)
        for m in range(team, members):
            my_block = jnp.where(idx[owners_at + m] == idx[member_at], m // team, my_block)
        lane = lax.broadcasted_iota(jnp.int32, (8, 128), 1)
        row = lax.broadcasted_iota(jnp.int32, (8, 128), 0)
        norms = jnp.where(lane == blocks + my_block, jnp.sum(prod * prod), sref[...])
        high = norms.astype(bf16).astype(f32)
        rest = norms - high
        mid = rest.astype(bf16).astype(f32)
        low = rest - mid
        tail = jnp.where(row == 0, high, jnp.where(row == 1, mid, jnp.where(row == 2, low, 0.0)))
        small = prod.astype(bf16)
        to = lax.broadcasted_iota(jnp.int32, (members * 8, held), 0)
        of = lax.broadcasted_iota(jnp.int32, (members * 8, held), 1)
        base = (of // share) * 8 + lax.rem(of, share)
        placed = jnp.zeros((members * 8, 128), f32)
        for x in range(tiles):
            pick = (to == base + x * share).astype(bf16)
            placed += jnp.dot(
                pick, small[:, x * 128 : (x + 1) * 128], preferred_element_type=f32
            )
        out[:, :8, :] = placed.reshape(members, 8, 128).astype(bf16)
        out[:, 8:, :] = jnp.broadcast_to(tail[None], (members, 8, 128)).astype(bf16)

    return call(
        body,
        "left_product",
        [SMEM, VMEM, VMEM, VMEM],
        jax.ShapeDtypeStruct((members, 16, 128), bf16),
    )(scalars, left, columns, squares)


def finish(returned, scalars, owners_at, rows, width, blocks):
    members = returned.shape[0]
    tiles = width // blocks // 128
    team = members // blocks
    share = rows // team
    count = team * 8

    def body(idx, got, out, held):
        sums = jnp.sum(got[:, 8:, :].astype(f32), axis=0)
        sums = jnp.sum(sums, axis=0, keepdims=True)
        lane = lax.broadcasted_iota(jnp.int32, (1, 128), 1)
        to = lax.broadcasted_iota(jnp.int32, (count, count), 0)
        of = lax.broadcasted_iota(jnp.int32, (count, count), 1)
        inner = lax.rem(to, rows)
        pick = (of == (inner // share) * 8 + (to // rows) * share + lax.rem(inner, share)).astype(f32)
        for k in range(blocks):
            for i in range(team):
                m = k * team + i
                held[m] = got[idx[owners_at + m], :8, :].astype(f32)
            adam = jnp.sum(jnp.where(lane == k, sums, 0.0), axis=1, keepdims=True)
            shampoo = jnp.sum(jnp.where(lane == blocks + k, sums, 0.0), axis=1, keepdims=True)
            ratio = jnp.sqrt(adam / (shampoo + 1e-06))
            flat = held[k * team : (k + 1) * team].reshape(count, 128).astype(bf16)
            moved = jnp.dot(pick.astype(bf16), flat, preferred_element_type=f32)
            for x in range(tiles):
                n = k * tiles + x
                tile = moved[x * rows : (x + 1) * rows] * ratio
                out[:, n * 128 : (n + 1) * 128] = tile.astype(bf16)

    return call(
        body,
        "finish",
        [SMEM, VMEM],
        jax.ShapeDtypeStruct((rows, width), bf16),
        [pltpu.VMEM((members, 8, 128), f32)],
    )(scalars, returned)


def local(gradients, second_moment, left_rows, right_root, owner_table, step_count):
    ny, nz = lax.axis_size("y"), lax.axis_size("z_hi")
    yi = lax.axis_index("y")
    members = lax.axis_size(FS)
    rows, width = gradients.shape[3], gradients.shape[4]
    size = right_root.shape[3]
    blocks = right_root.shape[1]
    sign = 1 - 2 * lax.axis_index("core")

    def along(value, turn):
        steps = (turn, -turn)
        pairs = [(c * ny + j, c * ny + (j + steps[c]) % ny) for c in range(2) for j in range(ny)]
        return lax.ppermute(value, ("core", "y"), pairs)

    def at(offset):
        return jnp.bitwise_and(yi + sign * offset + ny, ny - 1).astype(jnp.int32).reshape(1)

    owners = lax.dynamic_index_in_dim(owner_table, lax.axis_index(REP), 0, keepdims=False)
    scalars = jnp.concatenate([lax.axis_index(FS).reshape(1), step_count, owners]).astype(jnp.int32)
    member_at, step_at, owners_at = 0, 1, 2

    chunks = gradients.reshape(ny, nz, rows, width)
    four, two = take(chunks, at(4), at(2))
    four = along(four, 1)
    two = along(two, 1)
    three, minus_three, minus_two = ring_add(chunks, at(3), four, also=(at(-3), at(-2)))
    three = along(three, 2)
    minus_three = along(minus_three, -2)
    minus_two = along(minus_two, -1)
    one = along(ring_add(chunks, at(1), two, three), 1)
    minus_one = along(ring_add(chunks, at(-1), minus_two, minus_three), -1)
    part = ring_add(chunks, at(0), one, minus_one, after=scalars)

    parts = lax.all_to_all(part, "z_hi", 0, 0, tiled=True)
    pieces, new_moment, squares = right_and_adam(
        parts, right_root[0], second_moment[0, 0], scalars, step_at, owners_at, members
    )
    columns = lax.all_to_all(pieces, FS, 0, 0, tiled=True).reshape(members * rows, size)
    sent = left_product(
        left_rows[0, 0], columns, squares, scalars, member_at, owners_at, blocks
    )
    returned = lax.all_to_all(sent, FS, 0, 0, tiled=True)
    update = finish(returned, scalars, owners_at, rows, width, blocks)
    return (update[None, None], new_moment[None, None])


def solution(mesh):
    fine = Mesh(mesh.devices.reshape(4, 4, 2, 8, 4), FS + REP)
    return jax.shard_map(
        local,
        mesh=fine,
        in_specs=(
            P(REP, FS, None, None, None),
            P(FS, REP, None, None),
            P(REP, FS, None, None),
            P(REP, None, None, None),
            P(),
            P(),
        ),
        out_specs=(P(FS, REP, None, None), P(FS, REP, None, None)),
        check_vma=False,
    )
```

```python
import math

import jax
import jax.numpy as jnp
from jax import lax
from jax.experimental import pallas as pl
from jax.experimental.pallas import tpu as pltpu
from jax.sharding import Mesh, PartitionSpec as P

beta_two = 0.95
adam_eps = 1e-08
log_beta = math.log(beta_two)
FS = ("z_lo", "x", "core")
REP = ("y", "z_hi")
f32 = jnp.float32
bf16 = jnp.bfloat16
VMEM_LIMIT = 24 * 1024 * 1024
SMEM = pl.BlockSpec(memory_space=pltpu.SMEM)
VMEM = pl.BlockSpec(memory_space=pltpu.VMEM)


def call(body, name, ins, outs, scratch=()):
    return pl.pallas_call(
        body,
        in_specs=ins,
        out_specs=jax.tree.map(lambda _: VMEM, outs),
        out_shape=outs,
        scratch_shapes=scratch,
        compiler_params=pltpu.CompilerParams(vmem_limit_bytes=VMEM_LIMIT),
        name=name,
    )


def take(chunks, *places):
    _, parts, rows, width = chunks.shape
    count = len(places)

    def body(*refs):
        ins, outs = refs[count : 2 * count], refs[2 * count :]
        for got, out in zip(ins, outs):
            out[...] = got[0]

    def block_at(n):
        return pl.BlockSpec((1, parts, rows, width), lambda g, *idx: (idx[n][0], 0, 0, 0))

    shape = jax.ShapeDtypeStruct((parts, rows, width), bf16)
    return pl.pallas_call(
        body,
        grid_spec=pltpu.PrefetchScalarGridSpec(
            num_scalar_prefetch=count,
            grid=(1,),
            in_specs=[block_at(n) for n in range(count)],
            out_specs=[pl.BlockSpec((parts, rows, width), lambda g, *idx: (0, 0, 0))] * count,
        ),
        out_shape=[shape] * count,
        compiler_params=pltpu.CompilerParams(vmem_limit_bytes=VMEM_LIMIT),
        name="take",
    )(*places, *[chunks] * count)


def ring_add(chunks, index, *received, after=None):
    _, parts, rows, width = chunks.shape
    half = parts // 2
    count = len(received)

    def body(idx, own, *refs):
        total = own[0].astype(f32)
        for got in refs[:count]:
            total = total + got[...].astype(f32)
        refs[-1][...] = total.astype(bf16)

    block = pl.BlockSpec((half, rows, width), lambda i, idx: (i, 0, 0))
    extra = [] if after is None else [after]
    return pl.pallas_call(
        body,
        grid_spec=pltpu.PrefetchScalarGridSpec(
            num_scalar_prefetch=1,
            grid=(2,),
            in_specs=[pl.BlockSpec((1, half, rows, width), lambda i, idx: (idx[0], i, 0, 0))]
            + [block] * count
            + [SMEM] * len(extra),
            out_specs=block,
        ),
        out_shape=jax.ShapeDtypeStruct((parts, rows, width), bf16),
        compiler_params=pltpu.CompilerParams(vmem_limit_bytes=VMEM_LIMIT),
        name="ring_add",
    )(index, chunks, *received, *extra)


def right_and_adam(parts, right, moment, scalars, step_at, owners_at, members):
    count, rows, width = parts.shape
    blocks, size, _ = right.shape
    team = members // blocks

    def body(idx, got, root, old, pieces, new, squares):
        total = got[0].astype(f32)
        for i in range(1, count):
            total = total + got[i].astype(f32)
        grad = total.astype(bf16)
        for k in range(blocks):
            prod = jnp.dot(
                grad[:, k * size : (k + 1) * size], root[k], preferred_element_type=f32
            ).astype(bf16)
            for i in range(team):
                pieces[idx[owners_at + k * team + i]] = prod
        steps = jnp.full((8, 128), idx[step_at], jnp.int32).astype(f32)
        correction = (1.0 - jnp.exp(steps * log_beta))[:1, :1]
        m = beta_two * old[...] + (1.0 - beta_two) * total * total
        new[...] = m
        d = total / (jnp.sqrt(m / correction) + adam_eps)
        d = d * d
        lane = lax.broadcasted_iota(jnp.int32, (8, 128), 1)
        acc = jnp.zeros((8, 128), f32)
        for k in range(blocks):
            acc = jnp.where(lane == k, jnp.sum(d[:, k * size : (k + 1) * size]), acc)
        squares[...] = acc

    shapes = (
        jax.ShapeDtypeStruct((members, rows, size), bf16),
        jax.ShapeDtypeStruct((rows, width), f32),
        jax.ShapeDtypeStruct((8, 128), f32),
    )
    return call(body, "right_and_adam", [SMEM, VMEM, VMEM, VMEM], shapes)(
        scalars, parts, right, moment
    )


def left_product(left, columns, squares, scalars, member_at, owners_at, blocks):
    held, size = left.shape
    tiles = size // 128
    share = 8 // tiles
    members = held // share
    team = members // blocks

    def body(idx, lref, cref, sref, out):
        prod = jnp.dot(lref[...], cref[...], preferred_element_type=f32)
        my_block = jnp.int32(0)
        for m in range(team, members):
            my_block = jnp.where(idx[owners_at + m] == idx[member_at], m // team, my_block)
        lane = lax.broadcasted_iota(jnp.int32, (8, 128), 1)
        row = lax.broadcasted_iota(jnp.int32, (8, 128), 0)
        norms = jnp.where(lane == blocks + my_block, jnp.sum(prod * prod), sref[...])
        high = norms.astype(bf16).astype(f32)
        rest = norms - high
        mid = rest.astype(bf16).astype(f32)
        low = rest - mid
        tail = jnp.where(row == 0, high, jnp.where(row == 1, mid, jnp.where(row == 2, low, 0.0)))
        small = prod.astype(bf16)
        to = lax.broadcasted_iota(jnp.int32, (members * 8, held), 0)
        of = lax.broadcasted_iota(jnp.int32, (members * 8, held), 1)
        base = (of // share) * 8 + lax.rem(of, share)
        placed = jnp.zeros((members * 8, 128), f32)
        for x in range(tiles):
            pick = (to == base + x * share).astype(bf16)
            placed += jnp.dot(
                pick, small[:, x * 128 : (x + 1) * 128], preferred_element_type=f32
            )
        out[:, :8, :] = placed.reshape(members, 8, 128).astype(bf16)
        out[:, 8:, :] = jnp.broadcast_to(tail[None], (members, 8, 128)).astype(bf16)

    return call(
        body,
        "left_product",
        [SMEM, VMEM, VMEM, VMEM],
        jax.ShapeDtypeStruct((members, 16, 128), bf16),
    )(scalars, left, columns, squares)


def finish(returned, scalars, owners_at, rows, width, blocks):
    members = returned.shape[0]
    tiles = width // blocks // 128
    team = members // blocks
    share = rows // team
    count = team * 8

    def body(idx, got, out, held):
        sums = jnp.sum(got[:, 8:, :].astype(f32), axis=0)
        sums = jnp.sum(sums, axis=0, keepdims=True)
        lane = lax.broadcasted_iota(jnp.int32, (1, 128), 1)
        to = lax.broadcasted_iota(jnp.int32, (count, count), 0)
        of = lax.broadcasted_iota(jnp.int32, (count, count), 1)
        inner = lax.rem(to, rows)
        pick = (of == (inner // share) * 8 + (to // rows) * share + lax.rem(inner, share)).astype(f32)
        for k in range(blocks):
            for i in range(team):
                m = k * team + i
                held[m] = got[idx[owners_at + m], :8, :].astype(f32)
            adam = jnp.sum(jnp.where(lane == k, sums, 0.0), axis=1, keepdims=True)
            shampoo = jnp.sum(jnp.where(lane == blocks + k, sums, 0.0), axis=1, keepdims=True)
            ratio = jnp.sqrt(adam / (shampoo + 1e-06))
            flat = held[k * team : (k + 1) * team].reshape(count, 128).astype(bf16)
            moved = jnp.dot(pick.astype(bf16), flat, preferred_element_type=f32)
            for x in range(tiles):
                n = k * tiles + x
                tile = moved[x * rows : (x + 1) * rows] * ratio
                out[:, n * 128 : (n + 1) * 128] = tile.astype(bf16)

    return call(
        body,
        "finish",
        [SMEM, VMEM],
        jax.ShapeDtypeStruct((rows, width), bf16),
        [pltpu.VMEM((members, 8, 128), f32)],
    )(scalars, returned)


def local(gradients, second_moment, left_rows, right_root, owner_table, step_count):
    ny, nz = lax.axis_size("y"), lax.axis_size("z_hi")
    yi = lax.axis_index("y")
    members = lax.axis_size(FS)
    rows, width = gradients.shape[3], gradients.shape[4]
    size = right_root.shape[3]
    blocks = right_root.shape[1]
    sign = 1 - 2 * lax.axis_index("core")

    def along(value, turn):
        steps = (turn, -turn)
        pairs = [(c * ny + j, c * ny + (j + steps[c]) % ny) for c in range(2) for j in range(ny)]
        return lax.ppermute(value, ("core", "y"), pairs)

    def at(offset):
        return jnp.bitwise_and(yi + sign * offset + ny, ny - 1).astype(jnp.int32).reshape(1)

    owners = lax.dynamic_index_in_dim(owner_table, lax.axis_index(REP), 0, keepdims=False)
    scalars = jnp.concatenate([lax.axis_index(FS).reshape(1), step_count, owners]).astype(jnp.int32)
    member_at, step_at, owners_at = 0, 1, 2

    chunks = gradients.reshape(ny, nz, rows, width)
    four, minus_three, two, minus_two = take(chunks, at(4), at(-3), at(2), at(-2))
    four = along(four, 1)
    minus_three = along(minus_three, -2)
    two = along(two, 1)
    minus_two = along(minus_two, -1)
    three = along(ring_add(chunks, at(3), four, after=scalars), 2)
    minus_one = along(ring_add(chunks, at(-1), minus_two, minus_three), -1)
    one = along(ring_add(chunks, at(1), two, three), 1)
    part = ring_add(chunks, at(0), one, minus_one)

    parts = lax.all_to_all(part, "z_hi", 0, 0, tiled=True)
    pieces, new_moment, squares = right_and_adam(
        parts, right_root[0], second_moment[0, 0], scalars, step_at, owners_at, members
    )
    columns = lax.all_to_all(pieces, FS, 0, 0, tiled=True).reshape(members * rows, size)
    sent = left_product(
        left_rows[0, 0], columns, squares, scalars, member_at, owners_at, blocks
    )
    returned = lax.all_to_all(sent, FS, 0, 0, tiled=True)
    update = finish(returned, scalars, owners_at, rows, width, blocks)
    return (update[None, None], new_moment[None, None])


def solution(mesh):
    fine = Mesh(mesh.devices.reshape(4, 4, 2, 8, 4), FS + REP)
    return jax.shard_map(
        local,
        mesh=fine,
        in_specs=(
            P(REP, FS, None, None, None),
            P(FS, REP, None, None),
            P(REP, FS, None, None),
            P(REP, None, None, None),
            P(),
            P(),
        ),
        out_specs=(P(FS, REP, None, None), P(FS, REP, None, None)),
        check_vma=False,
    )
```

```python
import math

import jax
import jax.numpy as jnp
from jax import lax
from jax.experimental import pallas as pl
from jax.experimental.pallas import tpu as pltpu
from jax.sharding import Mesh, PartitionSpec as P

beta_two = 0.95
adam_eps = 1e-08
log_beta = math.log(beta_two)
FS = ("z_lo", "x", "core")
REP = ("y", "z_hi")
f32 = jnp.float32
bf16 = jnp.bfloat16
VMEM_LIMIT = 24 * 1024 * 1024
SMEM = pl.BlockSpec(memory_space=pltpu.SMEM)
VMEM = pl.BlockSpec(memory_space=pltpu.VMEM)


def call(body, name, ins, outs, scratch=()):
    return pl.pallas_call(
        body,
        in_specs=ins,
        out_specs=jax.tree.map(lambda _: VMEM, outs),
        out_shape=outs,
        scratch_shapes=scratch,
        compiler_params=pltpu.CompilerParams(vmem_limit_bytes=VMEM_LIMIT),
        name=name,
    )


def take(chunks, *places):
    _, parts, rows, width = chunks.shape
    count = len(places)

    def body(*refs):
        ins, outs = refs[count : 2 * count], refs[2 * count :]
        for got, out in zip(ins, outs):
            out[...] = got[0]

    def block_at(n):
        return pl.BlockSpec((1, parts, rows, width), lambda g, *idx: (idx[n][0], 0, 0, 0))

    shape = jax.ShapeDtypeStruct((parts, rows, width), bf16)
    return pl.pallas_call(
        body,
        grid_spec=pltpu.PrefetchScalarGridSpec(
            num_scalar_prefetch=count,
            grid=(1,),
            in_specs=[block_at(n) for n in range(count)],
            out_specs=[pl.BlockSpec((parts, rows, width), lambda g, *idx: (0, 0, 0))] * count,
        ),
        out_shape=[shape] * count,
        compiler_params=pltpu.CompilerParams(vmem_limit_bytes=VMEM_LIMIT),
        name="take",
    )(*places, *[chunks] * count)


def ring_add(chunks, index, *received, after=None):
    _, parts, rows, width = chunks.shape
    half = parts // 2
    count = len(received)

    def body(idx, own, *refs):
        total = own[0].astype(f32)
        for got in refs[:count]:
            total = total + got[...].astype(f32)
        refs[-1][...] = total.astype(bf16)

    block = pl.BlockSpec((half, rows, width), lambda i, idx: (i, 0, 0))
    extra = [] if after is None else [after]
    return pl.pallas_call(
        body,
        grid_spec=pltpu.PrefetchScalarGridSpec(
            num_scalar_prefetch=1,
            grid=(2,),
            in_specs=[pl.BlockSpec((1, half, rows, width), lambda i, idx: (idx[0], i, 0, 0))]
            + [block] * count
            + [SMEM] * len(extra),
            out_specs=block,
        ),
        out_shape=jax.ShapeDtypeStruct((parts, rows, width), bf16),
        compiler_params=pltpu.CompilerParams(vmem_limit_bytes=VMEM_LIMIT),
        name="ring_add",
    )(index, chunks, *received, *extra)


def right_and_adam(parts, right, moment, scalars, step_at, owners_at, members):
    count, rows, width = parts.shape
    blocks, size, _ = right.shape
    team = members // blocks

    def body(idx, got, root, old, pieces, new, squares):
        total = got[0].astype(f32)
        for i in range(1, count):
            total = total + got[i].astype(f32)
        grad = total.astype(bf16)
        for k in range(blocks):
            prod = jnp.dot(
                grad[:, k * size : (k + 1) * size], root[k], preferred_element_type=f32
            ).astype(bf16)
            for i in range(team):
                pieces[idx[owners_at + k * team + i]] = prod
        steps = jnp.full((8, 128), idx[step_at], jnp.int32).astype(f32)
        correction = (1.0 - jnp.exp(steps * log_beta))[:1, :1]
        m = beta_two * old[...] + (1.0 - beta_two) * total * total
        new[...] = m
        d = total / (jnp.sqrt(m / correction) + adam_eps)
        d = d * d
        lane = lax.broadcasted_iota(jnp.int32, (8, 128), 1)
        acc = jnp.zeros((8, 128), f32)
        for k in range(blocks):
            acc = jnp.where(lane == k, jnp.sum(d[:, k * size : (k + 1) * size]), acc)
        squares[...] = acc

    shapes = (
        jax.ShapeDtypeStruct((members, rows, size), bf16),
        jax.ShapeDtypeStruct((rows, width), f32),
        jax.ShapeDtypeStruct((8, 128), f32),
    )
    return call(body, "right_and_adam", [SMEM, VMEM, VMEM, VMEM], shapes)(
        scalars, parts, right, moment
    )


def left_product(left, columns, squares, scalars, member_at, owners_at, blocks):
    held, size = left.shape
    tiles = size // 128
    share = 8 // tiles
    members = held // share
    team = members // blocks

    def body(idx, lref, cref, sref, out):
        prod = jnp.dot(lref[...], cref[...], preferred_element_type=f32)
        my_block = jnp.int32(0)
        for m in range(team, members):
            my_block = jnp.where(idx[owners_at + m] == idx[member_at], m // team, my_block)
        lane = lax.broadcasted_iota(jnp.int32, (8, 128), 1)
        row = lax.broadcasted_iota(jnp.int32, (8, 128), 0)
        norms = jnp.where(lane == blocks + my_block, jnp.sum(prod * prod), sref[...])
        high = norms.astype(bf16).astype(f32)
        rest = norms - high
        mid = rest.astype(bf16).astype(f32)
        low = rest - mid
        tail = jnp.where(row == 0, high, jnp.where(row == 1, mid, jnp.where(row == 2, low, 0.0)))
        small = prod.astype(bf16)
        to = lax.broadcasted_iota(jnp.int32, (members * 8, held), 0)
        of = lax.broadcasted_iota(jnp.int32, (members * 8, held), 1)
        base = (of // share) * 8 + lax.rem(of, share)
        placed = jnp.zeros((members * 8, 128), f32)
        for x in range(tiles):
            pick = (to == base + x * share).astype(bf16)
            placed += jnp.dot(
                pick, small[:, x * 128 : (x + 1) * 128], preferred_element_type=f32
            )
        out[:, :8, :] = placed.reshape(members, 8, 128).astype(bf16)
        out[:, 8:, :] = jnp.broadcast_to(tail[None], (members, 8, 128)).astype(bf16)

    return call(
        body,
        "left_product",
        [SMEM, VMEM, VMEM, VMEM],
        jax.ShapeDtypeStruct((members, 16, 128), bf16),
    )(scalars, left, columns, squares)


def finish(returned, scalars, owners_at, rows, width, blocks):
    members = returned.shape[0]
    tiles = width // blocks // 128
    team = members // blocks
    share = rows // team
    count = team * 8

    def body(idx, got, out, held):
        sums = jnp.sum(got[:, 8:, :].astype(f32), axis=0)
        sums = jnp.sum(sums, axis=0, keepdims=True)
        lane = lax.broadcasted_iota(jnp.int32, (1, 128), 1)
        to = lax.broadcasted_iota(jnp.int32, (count, count), 0)
        of = lax.broadcasted_iota(jnp.int32, (count, count), 1)
        inner = lax.rem(to, rows)
        pick = (of == (inner // share) * 8 + (to // rows) * share + lax.rem(inner, share)).astype(f32)
        for k in range(blocks):
            for i in range(team):
                m = k * team + i
                held[m] = got[idx[owners_at + m], :8, :].astype(f32)
            adam = jnp.sum(jnp.where(lane == k, sums, 0.0), axis=1, keepdims=True)
            shampoo = jnp.sum(jnp.where(lane == blocks + k, sums, 0.0), axis=1, keepdims=True)
            ratio = jnp.sqrt(adam / (shampoo + 1e-06))
            flat = held[k * team : (k + 1) * team].reshape(count, 128).astype(bf16)
            moved = jnp.dot(pick.astype(bf16), flat, preferred_element_type=f32)
            for x in range(tiles):
                n = k * tiles + x
                tile = moved[x * rows : (x + 1) * rows] * ratio
                out[:, n * 128 : (n + 1) * 128] = tile.astype(bf16)

    return call(
        body,
        "finish",
        [SMEM, VMEM],
        jax.ShapeDtypeStruct((rows, width), bf16),
        [pltpu.VMEM((members, 8, 128), f32)],
    )(scalars, returned)


def local(gradients, second_moment, left_rows, right_root, owner_table, step_count):
    ny, nz = lax.axis_size("y"), lax.axis_size("z_hi")
    yi = lax.axis_index("y")
    members = lax.axis_size(FS)
    rows, width = gradients.shape[3], gradients.shape[4]
    size = right_root.shape[3]
    blocks = right_root.shape[1]
    sign = 1 - 2 * lax.axis_index("core")

    def along(value, turn):
        steps = (turn, -turn)
        pairs = [(c * ny + j, c * ny + (j + steps[c]) % ny) for c in range(2) for j in range(ny)]
        return lax.ppermute(value, ("core", "y"), pairs)

    def at(offset):
        return jnp.bitwise_and(yi + sign * offset + ny, ny - 1).astype(jnp.int32).reshape(1)

    owners = lax.dynamic_index_in_dim(owner_table, lax.axis_index(REP), 0, keepdims=False)
    scalars = jnp.concatenate([lax.axis_index(FS).reshape(1), step_count, owners]).astype(jnp.int32)
    member_at, step_at, owners_at = 0, 1, 2

    chunks = gradients.reshape(ny, nz, rows, width)
    four, minus_three, two, minus_two = take(chunks, at(4), at(-3), at(2), at(-2))
    four = along(four, 1)
    minus_three = along(minus_three, -2)
    two = along(two, 1)
    minus_two = along(minus_two, -1)
    three = along(ring_add(chunks, at(3), four), 2)
    minus_one = along(ring_add(chunks, at(-1), minus_two, minus_three), -1)
    one = along(ring_add(chunks, at(1), two, three), 1)
    part = ring_add(chunks, at(0), one, minus_one, after=scalars)

    parts = lax.all_to_all(part, "z_hi", 0, 0, tiled=True)
    pieces, new_moment, squares = right_and_adam(
        parts, right_root[0], second_moment[0, 0], scalars, step_at, owners_at, members
    )
    columns = lax.all_to_all(pieces, FS, 0, 0, tiled=True).reshape(members * rows, size)
    sent = left_product(
        left_rows[0, 0], columns, squares, scalars, member_at, owners_at, blocks
    )
    returned = lax.all_to_all(sent, FS, 0, 0, tiled=True)
    update = finish(returned, scalars, owners_at, rows, width, blocks)
    return (update[None, None], new_moment[None, None])


def solution(mesh):
    fine = Mesh(mesh.devices.reshape(4, 4, 2, 8, 4), FS + REP)
    return jax.shard_map(
        local,
        mesh=fine,
        in_specs=(
            P(REP, FS, None, None, None),
            P(FS, REP, None, None),
            P(REP, FS, None, None),
            P(REP, None, None, None),
            P(),
            P(),
        ),
        out_specs=(P(FS, REP, None, None), P(FS, REP, None, None)),
        check_vma=False,
    )
```
